128 devices in a mesh: pp: 8 (over y, core), ep: 16 (over z, x).
Axes of the slice: x: 4, y: 4, z: 4, core: 2. Of those that a mesh axis runs over, the one named last changes fastest.
Arguments:
- in_flight: bfloat16 [2, 8, 2048, 3584], P(None, 'pp', 'ep'), may hold values from -6 to 6
- routes: int32 [2, 2, 8, 2048, 2], P(None, None, 'pp', 'ep'), may hold values from 0 to 7, all different within a row; in each aligned block of 128 rows (0 to 127, 128 to 255, ..., all dimensions but the last counted through in order) at most 40 rows name the same one
- gate_weights: float32 [2, 2, 8, 2048, 2], P(None, None, 'pp', 'ep'), may hold values from 0.2 to 1.25
- norm_gain: float32 [2, 8, 3584], P(None, 'pp'), may hold values from 0.1 to 1.9
- w_gate: bfloat16 [2, 8, 3584, 8192], P(None, 'pp', None, 'ep'), may hold values from -0.09375 to 0.09375
- w_up: bfloat16 [2, 8, 3584, 8192], P(None, 'pp', None, 'ep'), may hold values from -0.09375 to 0.09375
- w_down: bfloat16 [2, 8, 8192, 3584], P(None, 'pp', 'ep'), may hold values from -0.1875 to 0.1875
Outputs:
- section_out: bfloat16 [2, 8, 2048, 3584], P(None, 'pp', 'ep')
The draws below stay inside these ranges and needn't reach their ends.
Inputs may be any that keep to these rules, and one draw needn't show every extreme that they name: `routes`: the 2 ids of a row differ. In each aligned block of 128 rows (the tokens of one device at one step and section) no expert is named by more than 40 rows, a bound that some block reaches.
All inputs are finite; a program needn't handle non-finite values.
Results may differ from the reference program's by a relative error of at most 0.0076.
Values may be sent and summed in bfloat16 or wider, within the bound.
No kernel may reach another device: no remote copies, remote signals or barrier semaphores. Data moves between devices by JAX's collectives and lax.ppermute only.
A program may use at most 128 MiB of HBM per device.

```python
import math
import jax
import jax.numpy as jnp
import numpy as np
from jax import lax

D = 3584
FE = 1024
TOPK = 2
TICKS = 2
TOK_DEV = 128
EXPERTS = 8
CAP = 40
TOKENS_MB = 2048
N_PP = 8


def block_levels(key, dims, split, least, high):
    level = 1.0
    for position, blocks in split:
        heights = jax.random.uniform(jax.random.fold_in(jax.random.fold_in(key, 6), position), (blocks,), jnp.float32, least / len(split), high / len(split))
        level = level * jnp.repeat(jnp.exp(heights), dims[position] // blocks).reshape((-1,) + (1,) * (len(dims) - 1 - position))
    return level


def shared_out(own_key, own, number, rows, number_of, top, most, skew):
    sequence = jax.random.permutation(own_key, number_of)
    packed, ordinary = shares(number_of, rows * top, most, skew, True), shares(number_of, rows * top, most, skew, False)
    places = jnp.arange(number_of)

    def named(lengths, turn):
        used = int((lengths > 0).sum())
        fixed = max(1, used // 4)
        moved = fixed + (places - fixed + turn * (used - fixed)) % max(1, number_of - fixed)
        return jnp.zeros((number_of,), jnp.int32).at[sequence[jnp.where(places < fixed, places, moved)]].set(jnp.asarray(lengths, jnp.int32))

    lengths = jnp.where(number % 4 == 0, named(packed, number // 4), named(ordinary, number - number // 4 - 1))
    mixed = jax.random.permutation(jax.random.fold_in(own, 3), number_of)
    source_of, sink = mixed[0:number_of // 2 * 2:2], mixed[1:number_of // 2 * 2:2]
    room = jnp.minimum(lengths[source_of] - 1, most - lengths[sink]) // 2
    room = jnp.where((source_of == sequence[0]) | (sink == sequence[0]) | (lengths[sink] == 0), 0, jnp.maximum(room, 0))
    moved = jax.random.randint(jax.random.fold_in(own, 4), (number_of // 2,), 0, 1 << 20) % (room + 1)
    lengths = lengths.at[source_of].add(-moved).at[sink].add(moved)
    members = jnp.searchsorted(jnp.cumsum(lengths), jnp.arange(rows * top), side="right").astype(jnp.int32)
    table = members.reshape(top, rows).T
    table = table[jax.random.permutation(jax.random.fold_in(own, 1), rows)]
    turn = jax.random.randint(jax.random.fold_in(own, 2), (rows, 1), 0, top)
    return jnp.take_along_axis(table, (jnp.arange(top)[None, :] + turn) % top, axis=1)


def shares(amount, total, most, skew, full):
    portions = [(1 << 20) // math.isqrt(rank ** skew) + 1 for rank in range(1, amount + 1)]
    largest = most if full else min(most, max(-(-total // amount), total * portions[0] // sum(portions)))
    least = 1 if total - largest >= amount - 1 else 0
    given, surplus = [largest] + [least] * (amount - 1), total - largest - least * (amount - 1)
    while surplus > 0:
        candidates = [i for i in range(1, amount) if given[i] < largest] or [i for i in range(1, amount) if given[i] < most]
        mass, budget = sum([portions[i] for i in candidates]), surplus
        for i in candidates:
            extra = min(most - given[i], max(1, budget * portions[i] // mass), surplus)
            given[i] = given[i] + extra
            surplus = surplus - extra
    return np.array(given)


def gaussian(stream_key, shape, scale, reach, shards=(), kind=jnp.bfloat16):
    drawn = scale * jax.random.normal(stream_key, shape, jnp.float32)
    if shards:
        drawn = drawn * block_levels(stream_key, shape, shards, -0.22, 0.18)
    return jnp.clip(drawn, -reach, reach).astype(kind)


def setup_inputs(seed: int = 0) -> dict:
    streams_of = jax.random.split(jax.random.key(seed), 8)
    in_flight = gaussian(streams_of[0], (2, N_PP, TOKENS_MB, D), 1.0, 6.0, ((1, 8), (2, 16)))
    routes_keys = jax.random.split(jax.random.fold_in(streams_of[1], 1), TICKS * 2 * N_PP * TOKENS_MB // TOK_DEV)
    routes_turns = jax.random.permutation(jax.random.fold_in(streams_of[1], 3), TICKS * 2 * N_PP * TOKENS_MB // TOK_DEV)
    routes = jax.vmap(lambda own, number: shared_out(jax.random.fold_in(streams_of[1], 2), own, number, TOK_DEV, EXPERTS, TOPK, CAP, 1))(routes_keys, routes_turns).reshape((TICKS, 2, N_PP, TOKENS_MB, TOPK))
    gate_weights = jnp.clip(0.2 + 1.05 * jax.random.uniform(streams_of[2], (TICKS, 2, N_PP, TOKENS_MB, TOPK), jnp.float32) ** block_levels(streams_of[2], (TICKS, 2, N_PP, TOKENS_MB, TOPK), ((2, 8), (3, 16)), -0.2, 0.2), 0.2, 1.25)
    norm_gain = jnp.clip(1.0 + 0.18 * jax.random.normal(streams_of[3], (2, N_PP, D), jnp.float32), 0.1, 1.9)
    w_gate = gaussian(streams_of[4], (2, N_PP, D, EXPERTS * FE), D ** -0.5, 0.09375, ((1, 8), (3, 16)))
    w_up = gaussian(streams_of[5], (2, N_PP, D, EXPERTS * FE), D ** -0.5, 0.09375, ((1, 8), (3, 16)))
    w_down = gaussian(streams_of[6], (2, N_PP, EXPERTS * FE, D), FE ** -0.5, 0.1875, ((1, 8), (2, 16)))
    return dict(in_flight=in_flight, routes=routes, gate_weights=gate_weights, norm_gain=norm_gain, w_gate=w_gate, w_up=w_up, w_down=w_down)


def run_section(values, route_ids, route_weights, gain_row, gate_cols, up_cols, down_rows):
    total_rows = values.shape[0]
    blocks = total_rows // TOK_DEV
    widened = values.astype(jnp.float32)
    normed = (widened * lax.rsqrt(lax.optimization_barrier(jnp.mean(widened * widened, axis=-1, keepdims=True)) + 1e-06) * gain_row).astype(jnp.bfloat16)
    flat_ids = route_ids.reshape(blocks, TOK_DEV * TOPK).astype(jnp.int32)
    onehot = (flat_ids[:, :, None] == jnp.arange(EXPERTS, dtype=jnp.int32)[None, None, :]).astype(jnp.int32)
    slot_index = lax.optimization_barrier(jnp.sum((jnp.cumsum(onehot, axis=1) - 1) * onehot, axis=-1)).astype(jnp.int32)
    token_index = jnp.broadcast_to((jnp.arange(TOK_DEV * TOPK, dtype=jnp.int32) // TOPK)[None, :], flat_ids.shape)
    block_index = jnp.broadcast_to(jnp.arange(blocks, dtype=jnp.int32)[:, None], flat_ids.shape)
    source_rows = normed.reshape(blocks, TOK_DEV, D)[block_index, token_index]
    buffer = jnp.zeros((EXPERTS, blocks, CAP, D), jnp.bfloat16).at[flat_ids, block_index, slot_index].set(source_rows)
    half_width = FE // 2
    outputs = []
    for expert in range(EXPERTS):
        expert_rows = buffer[expert].reshape(blocks * CAP, D)
        summed = jnp.zeros((blocks * CAP, D), jnp.float32)
        for half_index in range(2):
            col_start = expert * FE + half_index * half_width
            gate_val = jnp.dot(expert_rows, gate_cols[:, col_start:col_start + half_width], preferred_element_type=jnp.float32)
            up_val = jnp.dot(expert_rows, up_cols[:, col_start:col_start + half_width], preferred_element_type=jnp.float32)
            active = (jax.nn.silu(gate_val) * up_val).astype(jnp.bfloat16)
            partial_out = jnp.dot(active, down_rows[col_start:col_start + half_width], preferred_element_type=jnp.float32).astype(jnp.bfloat16)
            partial_out = lax.optimization_barrier(partial_out)
            summed = summed + partial_out.astype(jnp.float32)
        expert_out = lax.optimization_barrier(summed.astype(jnp.bfloat16))
        outputs.append(expert_out.reshape(blocks, CAP, D))
    results = jnp.stack(outputs)
    picked = results[flat_ids, block_index, slot_index].astype(jnp.float32)
    weighted = picked * route_weights.reshape(blocks, TOK_DEV * TOPK)[:, :, None].astype(jnp.float32)
    mixture = lax.optimization_barrier(jnp.sum(weighted.reshape(total_rows, TOPK, D), axis=1))
    return (widened + mixture).astype(jnp.bfloat16)

def reference(in_flight, routes, gate_weights, norm_gain, w_gate, w_up, w_down):

    def apply_section(tick_index, leg_index, device_index, values):
        return run_section(values, routes[tick_index, leg_index, device_index], gate_weights[tick_index, leg_index, device_index], norm_gain[leg_index, device_index], w_gate[leg_index, device_index], w_up[leg_index, device_index], w_down[leg_index, device_index])
    places = [(0, section_index) if section_index < N_PP else (1, 2 * N_PP - 1 - section_index) for section_index in range(2 * N_PP)]
    first_tick = [apply_section(0, leg_index, device_index, in_flight[leg_index, device_index]) for leg_index, device_index in places]
    last_tick = {}
    last_tick[0, 0] = first_tick[2 * N_PP - 1]
    for section_index in range(1, 2 * N_PP):
        leg_index, device_index = places[section_index]
        last_tick[leg_index, device_index] = apply_section(1, leg_index, device_index, first_tick[section_index - 1])
    return jnp.stack([jnp.stack([last_tick[leg_index, device_index] for device_index in range(N_PP)]) for leg_index in range(2)])
```

```python
import functools

import jax
import jax.numpy as jnp
from jax import lax
from jax.experimental import pallas as pl
from jax.experimental.pallas import tpu as pltpu
from jax.sharding import PartitionSpec as P

SIDE = 4
COLUMNS = (
    [SIDE * z + x for z in range(SIDE) for x in (0, 3)],
    [SIDE * z + x for z in range(SIDE) for x in (1, 2)],
)
EXPERTS = 2 * SIDE
ROOM = 40 * 2**20
VMEM = pl.BlockSpec(memory_space=pltpu.VMEM)


def from_behind(value, axis, steps):
    count = lax.axis_size(axis)
    leading, last = (max(0, -steps), min(count, count - steps))
    return lax.ppermute(value, axis, [(source, source + steps) for source in range(leading, last)])


def other_half(value):
    return lax.ppermute(value, "ep", [(place, place ^ 1) for place in range(lax.axis_size("ep"))])


def within_column(rows):
    shape = rows.shape
    moved = lax.all_to_all(
        rows.reshape(EXPERTS, shape[0] // EXPERTS, shape[1]),
        "ep",
        split_axis=0,
        concat_axis=0,
        tiled=True,
        axis_index_groups=COLUMNS,
    )
    return moved.reshape(shape)


def iota(shape, dim):
    return lax.broadcasted_iota(jnp.int32, shape, dim)


def dot(left, right):
    return jnp.dot(left, right, preferred_element_type=jnp.float32)


def columns_of(width):
    return 512 if width % 512 == 0 else width


def normalise(value, gain):
    widened = value.astype(jnp.float32)
    scale = lax.rsqrt(jnp.mean(widened * widened, axis=-1, keepdims=True) + 1e-06)
    return (widened * scale * gain).astype(jnp.bfloat16)


def slot_by_row(ids):
    tokens = ids.shape[1]
    expert = iota((EXPERTS, tokens), 0)
    named = (ids[0:1] == expert) | (ids[1:2] == expert)
    before = (iota((tokens, tokens), 0) < iota((tokens, tokens), 1)).astype(jnp.bfloat16)
    earlier = dot(jnp.where(named, 1.0, 0.0).astype(jnp.bfloat16), before)
    return jnp.where(named, earlier, -1.0)


def dispatch_matrix(slot, capacity):
    tokens = slot.shape[1]
    place = iota((EXPERTS, capacity, tokens), 1).astype(jnp.float32)
    chosen = jnp.where(slot[:, None, :] == place, 1.0, 0.0)
    return chosen.reshape(EXPERTS * capacity, tokens).astype(jnp.bfloat16)


def combine_matrix(ids, weights, capacity, first, room):
    tokens = ids.shape[0]
    expert = iota((tokens, EXPERTS), 1)
    named = (ids[:, 0:1] == expert) | (ids[:, 1:2] == expert)
    before = (iota((tokens, tokens), 0) > iota((tokens, tokens), 1)).astype(jnp.bfloat16)
    earlier = dot(before, jnp.where(named, 1.0, 0.0).astype(jnp.bfloat16))
    slot = jnp.where(named, earlier + first, -1.0).astype(jnp.bfloat16)
    weight = jnp.where(ids[:, 0:1] == expert, weights[:, 0:1], 0.0) + jnp.where(
        ids[:, 1:2] == expert, weights[:, 1:2], 0.0
    )
    total = EXPERTS * room
    offset = iota((EXPERTS, total), 1) - room * iota((EXPERTS, total), 0)
    spread = ((offset >= 0) & (offset < room)).astype(jnp.bfloat16)
    offset_row = jnp.sum(
        jnp.where((offset >= 0) & (offset < room), offset, 0), axis=0, keepdims=True
    )
    chosen = dot(slot, spread) == offset_row.astype(jnp.float32)
    high = weight.astype(jnp.bfloat16)
    low = (weight - high.astype(jnp.float32)).astype(jnp.bfloat16)
    return (
        jnp.where(chosen, dot(high, spread), 0.0).astype(jnp.bfloat16),
        jnp.where(chosen, dot(low, spread), 0.0).astype(jnp.bfloat16),
    )


def norm_kernel(value_ref, gain_ref, out_ref):
    out_ref[...] = normalise(value_ref[...], gain_ref[...])


def norm_pack_kernel(capacity, value_ref, gain_ref, ids_ref, out_ref, normed_ref):
    normed_ref[...] = normalise(value_ref[...], gain_ref[...])
    matrix = dispatch_matrix(slot_by_row(ids_ref[...]), capacity)
    width = columns_of(out_ref.shape[1])
    for start in range(0, out_ref.shape[1], width):
        cols = slice(start, start + width)
        out_ref[:, cols] = dot(matrix, normed_ref[:, cols]).astype(jnp.bfloat16)


def pair_pack_kernel(capacity, own_ref, other_ref, ids_ref, other_ids_ref, out_ref):
    other_slot = slot_by_row(other_ids_ref[...])
    own = dispatch_matrix(slot_by_row(ids_ref[...]), 2 * capacity)
    other = dispatch_matrix(
        jnp.where(other_slot >= 0.0, other_slot + float(capacity), -1.0), 2 * capacity
    )
    width = columns_of(out_ref.shape[1])
    for start in range(0, out_ref.shape[1], width):
        cols = slice(start, start + width)
        out_ref[:, cols] = (dot(own, own_ref[:, cols]) + dot(other, other_ref[:, cols])).astype(
            jnp.bfloat16
        )


def expert_kernel(steps, rows_ref, gate_ref, up_ref, down_ref, out_ref, gate_sum, up_sum, active):
    step = pl.program_id(0)

    @pl.when(step == 0)
    def _():
        gate_sum[...] = dot(rows_ref[...], gate_ref[...])
        up_sum[...] = dot(rows_ref[...], up_ref[...])

    @pl.when((step > 0) & (step < steps))
    def _():
        gate_sum[...] += dot(rows_ref[...], gate_ref[...])
        up_sum[...] += dot(rows_ref[...], up_ref[...])

    @pl.when(step == steps - 1)
    def _():
        active[...] = (jax.nn.silu(gate_sum[...]) * up_sum[...]).astype(jnp.bfloat16)

    @pl.when(step >= steps)
    def _():
        out_ref[...] = dot(active[...], down_ref[...]).astype(jnp.bfloat16)


def combine_kernel(capacity, value_ref, rows_ref, ids_ref, weights_ref, out_ref):
    high, low = combine_matrix(ids_ref[...], weights_ref[...], capacity, 0.0, capacity)
    width = columns_of(out_ref.shape[1])
    for start in range(0, out_ref.shape[1], width):
        cols = slice(start, start + width)
        rows = rows_ref[:, cols]
        mixture = dot(high, rows) + dot(low, rows)
        out_ref[:, cols] = (value_ref[:, cols].astype(jnp.float32) + mixture).astype(jnp.bfloat16)


def pair_combine_kernel(
    capacity, rows_ref, ids_ref, weights_ref, other_ids_ref, other_weights_ref, own_ref, other_ref
):
    room = 2 * capacity
    high, low = combine_matrix(ids_ref[...], weights_ref[...], capacity, 0.0, room)
    other_high, other_low = combine_matrix(
        other_ids_ref[...], other_weights_ref[...], capacity, float(capacity), room
    )
    width = columns_of(own_ref.shape[1])
    for start in range(0, own_ref.shape[1], width):
        cols = slice(start, start + width)
        rows = rows_ref[:, cols]
        own_ref[:, cols] = dot(high, rows) + dot(low, rows)
        other_ref[:, cols] = (dot(other_high, rows) + dot(other_low, rows)).astype(jnp.bfloat16)


def params():
    return pltpu.CompilerParams(vmem_limit_bytes=ROOM)


def call(kernel, outs, args, scratch=()):
    return pl.pallas_call(
        kernel,
        out_shape=outs,
        in_specs=[VMEM] * len(args),
        out_specs=jax.tree.map(lambda _: VMEM, outs),
        scratch_shapes=scratch,
        compiler_params=params(),
    )(*args)


def array(*shape, dtype=jnp.bfloat16):
    return jax.ShapeDtypeStruct(shape, dtype)


def norm(value, gain):
    return call(norm_kernel, array(*value.shape), (value, gain))


def norm_pack(value, gain, ids, capacity):
    return call(
        functools.partial(norm_pack_kernel, capacity),
        array(EXPERTS * capacity, value.shape[1]),
        (value, gain, ids),
        (pltpu.VMEM(value.shape, jnp.bfloat16),),
    )


def pair_pack(own, other, ids, other_ids, capacity):
    return call(
        functools.partial(pair_pack_kernel, capacity),
        array(EXPERTS * 2 * capacity, own.shape[1]),
        (own, other, ids, other_ids),
    )


def combine(value, rows, ids, weights, capacity):
    return call(
        functools.partial(combine_kernel, capacity), array(*value.shape), (value, rows, ids, weights)
    )


def pair_combine(rows, ids, weights, other_ids, other_weights, capacity):
    shape = (ids.shape[0], rows.shape[1])
    return call(
        functools.partial(pair_combine_kernel, capacity),
        (array(*shape, dtype=jnp.float32), array(*shape)),
        (rows, ids, weights, other_ids, other_weights),
    )


def expert_pass(rows, leg, gate_cols, up_cols, down_rows):
    count, width = rows.shape
    hidden = gate_cols.shape[-1]
    block = columns_of(width)
    steps = width // block

    def early(step):
        return jnp.minimum(step, steps - 1)

    def late(step):
        return jnp.maximum(step - steps, 0)

    return pl.pallas_call(
        functools.partial(expert_kernel, steps),
        grid=(2 * steps,),
        out_shape=array(count, width),
        in_specs=[
            pl.BlockSpec((count, block), lambda step: (0, early(step))),
            pl.BlockSpec((None, None, block, hidden), lambda step: (leg, 0, early(step), 0)),
            pl.BlockSpec((None, None, block, hidden), lambda step: (leg, 0, early(step), 0)),
            pl.BlockSpec((None, None, hidden, block), lambda step: (leg, 0, 0, late(step))),
        ],
        out_specs=pl.BlockSpec((count, block), lambda step: (0, late(step))),
        scratch_shapes=(
            pltpu.VMEM((count, hidden), jnp.float32),
            pltpu.VMEM((count, hidden), jnp.float32),
            pltpu.VMEM((count, hidden), jnp.bfloat16),
        ),
        compiler_params=params(),
        cost_estimate=pl.CostEstimate(
            flops=6 * count * width * hidden,
            bytes_accessed=2 * (2 * count * width + 3 * width * hidden),
            transcendentals=count * hidden,
        ),
    )(rows, gate_cols, up_cols, down_rows)


def on_device(in_flight, routes, gate_weights, norm_gain, w_gate, w_up, w_down):
    section_count = lax.axis_size("pp")
    section_pos = lax.axis_index("pp")
    tokens, top_count = routes.shape[-2:]
    capacity = tokens * top_count * 5 // (4 * EXPERTS)
    ids = routes[:, :, 0]
    ids_across = jnp.swapaxes(ids, -1, -2)
    weights = gate_weights[:, :, 0]
    other_ids = other_half(jnp.stack([ids[0, 0], ids[1, 1]]))
    other_ids_across = jnp.swapaxes(other_ids, -1, -2)
    other_weights = other_half(jnp.stack([weights[0, 0], weights[1, 1]]))

    def experts(rows, leg):
        return expert_pass(rows, leg, w_gate, w_up, w_down)

    def step(tick, wide, wide_value, lean, lean_value):
        normed = norm(wide_value, norm_gain[wide])
        normed_other = other_half(normed)
        packed = norm_pack(lean_value, norm_gain[lean], ids_across[tick, lean], capacity)
        lean_own = within_column(packed)
        wide_packed = pair_pack(
            normed, normed_other, ids_across[tick, wide], other_ids_across[tick], capacity
        )
        wide_rows = within_column(wide_packed)
        lean_other = other_half(lean_own)
        part_own = experts(lean_own, lean)
        part_other = experts(lean_other, lean)
        part_back = other_half(part_other)
        wide_out = experts(wide_rows, wide)
        wide_back = within_column(wide_out)
        lean_out = (part_own.astype(jnp.float32) + part_back.astype(jnp.float32)).astype(
            jnp.bfloat16
        )
        lean_back = within_column(lean_out)
        mixed_own, mixed_other = pair_combine(
            wide_back,
            ids[tick, wide],
            weights[tick, wide],
            other_ids[tick],
            other_weights[tick],
            capacity,
        )
        mixed_back = other_half(mixed_other)
        wide_done = (
            wide_value.astype(jnp.float32) + (mixed_own + mixed_back.astype(jnp.float32))
        ).astype(jnp.bfloat16)
        lean_done = combine(
            lean_value, lean_back, ids[tick, lean], weights[tick, lean], capacity
        )
        return wide_done, lean_done

    first_down, first_up = step(0, 0, in_flight[0, 0], 1, in_flight[1, 0])
    descending = from_behind(first_down, "pp", 1)
    ascending = from_behind(first_up, "pp", -1)
    turned = jnp.where(section_pos == section_count - 1, first_down, ascending)
    second_up, second_down = step(1, 1, turned, 0, descending)
    leading = jnp.where(section_pos == 0, first_up, second_down)
    return jnp.stack([leading, second_up])[:, None]


def solution(mesh):
    placed = (
        P(None, "pp", "ep", None),
        P(None, None, "pp", "ep", None),
        P(None, None, "pp", "ep", None),
        P(None, "pp", None),
        P(None, "pp", None, "ep"),
        P(None, "pp", None, "ep"),
        P(None, "pp", "ep", None),
    )
    return jax.shard_map(
        on_device, mesh=mesh, in_specs=placed, out_specs=P(None, "pp", "ep", None), check_vma=False
    )
```

```python
import functools

import jax
import jax.numpy as jnp
from jax import lax
from jax.experimental import pallas as pl
from jax.experimental.pallas import tpu as pltpu
from jax.sharding import PartitionSpec as P

SIDE = 4
COLUMNS = (
    [SIDE * z + x for z in range(SIDE) for x in (0, 3)],
    [SIDE * z + x for z in range(SIDE) for x in (1, 2)],
)
EXPERTS = 2 * SIDE
ROOM = 62 * 2**20
VMEM = pl.BlockSpec(memory_space=pltpu.VMEM)
SMEM = pl.BlockSpec(memory_space=pltpu.SMEM)
ANY = pl.BlockSpec(memory_space=pl.ANY)


def moved(value, steps, crossed):
    sections, places = lax.axis_size("pp"), lax.axis_size("ep")
    if steps == 0:
        sources = [sections - 1]
    else:
        sources = [section for section in range(sections) if 0 <= section + steps < sections]
    pairs = [
        (section * places + place, (section + steps) * places + (place ^ crossed))
        for section in sources
        for place in range(places)
    ]
    return lax.ppermute(value, ("pp", "ep"), pairs)


def other_half(value):
    return lax.ppermute(value, "ep", [(place, place ^ 1) for place in range(lax.axis_size("ep"))])


def within_column(rows):
    shape = rows.shape
    received = lax.all_to_all(
        rows.reshape(EXPERTS, shape[0] // EXPERTS, shape[1]),
        "ep",
        split_axis=0,
        concat_axis=0,
        tiled=True,
        axis_index_groups=COLUMNS,
    )
    return received.reshape(shape)


def iota(shape, dim):
    return lax.broadcasted_iota(jnp.int32, shape, dim)


def dot(left, right):
    return jnp.dot(left, right, preferred_element_type=jnp.float32)


def dot_down(left, right):
    return lax.dot_general(left, right, (((0,), (0,)), ((), ())), preferred_element_type=jnp.float32)


def array(*shape, dtype=jnp.bfloat16):
    return jax.ShapeDtypeStruct(shape, dtype)


def split(width, parts):
    return width // parts if width % (128 * parts) == 0 else width


def params():
    return pltpu.CompilerParams(vmem_limit_bytes=ROOM)


def normalise(value, gain):
    widened = value.astype(jnp.float32)
    scale = lax.rsqrt(jnp.mean(widened * widened, axis=-1, keepdims=True) + 1e-06)
    return (widened * scale * gain).astype(jnp.bfloat16)


def slots(ids):
    tokens = ids.shape[1]
    expert = iota((EXPERTS, tokens), 0)
    named = (ids[0:1] == expert) | (ids[1:2] == expert)
    before = (iota((tokens, tokens), 0) < iota((tokens, tokens), 1)).astype(jnp.bfloat16)
    earlier = dot(jnp.where(named, 1.0, 0.0).astype(jnp.bfloat16), before)
    return jnp.where(named, earlier, -1.0)


def slot_matrix(ids, capacity, first, room, weights=None):
    tokens = ids.shape[1]
    slot = slots(ids)
    place = iota((EXPERTS, room, tokens), 1).astype(jnp.float32) - float(first)
    if weights is None:
        value = 1.0
    else:
        expert = iota((EXPERTS, tokens), 0)
        value = jnp.where(ids[0:1] == expert, weights[0:1], 0.0) + jnp.where(
            ids[1:2] == expert, weights[1:2], 0.0
        )
        value = value[:, None, :]
    chosen = (slot[:, None, :] == place) & (place >= 0.0)
    return jnp.where(chosen, value, 0.0).reshape(EXPERTS * room, tokens)


def two_terms(matrix):
    high = matrix.astype(jnp.bfloat16)
    return high, (matrix - high.astype(jnp.float32)).astype(jnp.bfloat16)


def across(matrix):
    rows, tokens = matrix.shape
    extra = -rows % 128
    if extra:
        matrix = jnp.concatenate([matrix, jnp.zeros((extra, tokens), matrix.dtype)], axis=0)
    return matrix.T[:, :rows]


def lean_pack_kernel(where, capacity, value_ref, gain_ref, ids_ref, out_ref, normed_ref, matrix_ref):
    @pl.when(pl.program_id(0) == 0)
    def _():
        normed_ref[...] = normalise(value_ref[...], gain_ref[...])
        matrix_ref[...] = slot_matrix(ids_ref[where], capacity, 0, capacity).astype(jnp.bfloat16)

    width = out_ref.shape[1]
    cols = pl.ds(pl.multiple_of(pl.program_id(0) * width, 128), width)
    out_ref[...] = dot(matrix_ref[...], normed_ref[:, cols]).astype(jnp.bfloat16)


def sum_pack_kernel(
    where,
    capacity,
    first_ref,
    second_ref,
    gain_ref,
    ids_ref,
    value_ref,
    out_ref,
    normed_ref,
    matrix_ref,
):
    @pl.when(pl.program_id(0) == 0)
    def _():
        value_ref[...] = sum_of(first_ref, second_ref)

    lean_pack_kernel(
        where, capacity, value_ref, gain_ref, ids_ref, out_ref, normed_ref, matrix_ref
    )


def wide_pack_kernel(
    where,
    capacity,
    own_ref,
    other_ref,
    gain_ref,
    ids_ref,
    other_ids_ref,
    after_ref,
    out_ref,
    normed_ref,
    matrix_ref,
):
    @pl.when(pl.program_id(0) == 0)
    def _():
        room = 2 * capacity
        tokens = own_ref.shape[0]
        normed_ref[:tokens] = normalise(own_ref[...], gain_ref[...])
        normed_ref[tokens:] = normalise(other_ref[...], gain_ref[...])
        matrix_ref[:, :tokens] = slot_matrix(ids_ref[where], capacity, 0, room).astype(jnp.bfloat16)
        matrix_ref[:, tokens:] = slot_matrix(other_ids_ref[where], capacity, capacity, room).astype(
            jnp.bfloat16
        )

    width = out_ref.shape[1]
    cols = pl.ds(pl.multiple_of(pl.program_id(0) * width, 128), width)
    out_ref[...] = dot(matrix_ref[...], normed_ref[:, cols]).astype(jnp.bfloat16)


def sum_of(first_ref, second_ref):
    total = first_ref[...].astype(jnp.float32) + second_ref[...].astype(jnp.float32)
    return total.astype(jnp.bfloat16)


def either_pack_kernel(
    where,
    capacity,
    flag_ref,
    own_ref,
    other_ref,
    own_first_ref,
    own_second_ref,
    other_first_ref,
    other_second_ref,
    gain_ref,
    ids_ref,
    other_ids_ref,
    after_ref,
    value_ref,
    out_ref,
    normed_ref,
    matrix_ref,
    picked_ref,
):
    first = pl.program_id(0) == 0

    @pl.when(first & (flag_ref[0] == 0))
    def _():
        value_ref[...] = own_ref[...]
        picked_ref[...] = other_ref[...]

    @pl.when(first & (flag_ref[0] != 0))
    def _():
        value_ref[...] = sum_of(own_first_ref, own_second_ref)
        picked_ref[...] = sum_of(other_first_ref, other_second_ref)

    wide_pack_kernel(
        where,
        capacity,
        value_ref,
        picked_ref,
        gain_ref,
        ids_ref,
        other_ids_ref,
        after_ref,
        out_ref,
        normed_ref,
        matrix_ref,
    )


def expert_kernel(
    leg,
    deep,
    wide,
    rows_ref,
    gate_ref,
    up_ref,
    down_ref,
    after_ref,
    out_ref,
    rows,
    gate_cols,
    up_cols,
    down_rows,
    results,
    gate_sum,
    up_sum,
    active,
    rows_in,
    gate_in,
    up_in,
    down_in,
    results_out,
):
    arriving = []
    for number, cols in enumerate(deep):
        arriving.append(
            (
                pltpu.make_async_copy(rows_ref.at[:, cols], rows.at[:, cols], rows_in.at[number]),
                pltpu.make_async_copy(
                    gate_ref.at[leg, 0, cols], gate_cols.at[cols], gate_in.at[number]
                ),
                pltpu.make_async_copy(up_ref.at[leg, 0, cols], up_cols.at[cols], up_in.at[number]),
            )
        )
    for number, cols in enumerate(wide):
        arriving.append(
            (
                pltpu.make_async_copy(
                    down_ref.at[leg, 0, :, cols], down_rows.at[:, cols], down_in.at[number]
                ),
            )
        )
    for copies in arriving:
        for copy in copies:
            copy.start()
    for number, cols in enumerate(deep):
        for copy in arriving[number]:
            copy.wait()
        gate = dot(rows[:, cols], gate_cols[cols])
        up = dot(rows[:, cols], up_cols[cols])
        if number > 0:
            gate = gate + gate_sum[...]
            up = up + up_sum[...]
        if number < len(deep) - 1:
            gate_sum[...] = gate
            up_sum[...] = up
        else:
            active[...] = (jax.nn.silu(gate) * up).astype(jnp.bfloat16)
    leaving = []
    for number, cols in enumerate(wide):
        for copy in arriving[len(deep) + number]:
            copy.wait()
        results[:, cols] = dot(active[...], down_rows[:, cols]).astype(jnp.bfloat16)
        copy = pltpu.make_async_copy(
            results.at[:, cols], out_ref.at[:, cols], results_out.at[number]
        )
        copy.start()
        leaving.append(copy)
    for copy in leaving:
        copy.wait()


def combine_kernel(
    where, capacity, value_ref, rows_ref, ids_ref, weights_ref, out_ref, matrix_ref
):
    tokens = out_ref.shape[0]

    @pl.when(pl.program_id(0) == 0)
    def _():
        matrix = slot_matrix(ids_ref[where], capacity, 0, capacity, weights_ref[where])
        matrix_ref[:tokens], matrix_ref[tokens:] = two_terms(across(matrix))

    terms = dot(matrix_ref[...], rows_ref[...])
    mixture = terms[:tokens] + terms[tokens:]
    out_ref[...] = (value_ref[...].astype(jnp.float32) + mixture).astype(jnp.bfloat16)


def last_combine_kernel(
    where,
    capacity,
    flag_ref,
    value_ref,
    rows_ref,
    ids_ref,
    weights_ref,
    instead_ref,
    held_ref,
    out_ref,
    matrix_ref,
):
    combine_kernel(where, capacity, value_ref, rows_ref, ids_ref, weights_ref, out_ref, matrix_ref)

    @pl.when(flag_ref[0] != 0)
    def _():
        out_ref[...] = instead_ref[...]


def pair_combine_kernel(
    where,
    capacity,
    value_ref,
    rows_ref,
    ids_ref,
    weights_ref,
    other_ids_ref,
    other_weights_ref,
    own_ref,
    other_ref,
    matrix_ref,
):
    tokens = own_ref.shape[0]

    @pl.when(pl.program_id(0) == 0)
    def _():
        room = 2 * capacity
        own = across(slot_matrix(ids_ref[where], capacity, 0, room, weights_ref[where]))
        other = across(
            slot_matrix(other_ids_ref[where], capacity, capacity, room, other_weights_ref[where])
        )
        matrix_ref[:tokens], matrix_ref[tokens : 2 * tokens] = two_terms(own)
        matrix_ref[2 * tokens : 3 * tokens], matrix_ref[3 * tokens :] = two_terms(other)

    terms = dot(matrix_ref[...], rows_ref[...])
    own = value_ref[...].astype(jnp.float32) + terms[:tokens] + terms[tokens : 2 * tokens]
    own_ref[...] = own.astype(own_ref.dtype)
    other = terms[2 * tokens : 3 * tokens] + terms[3 * tokens :]
    other_ref[...] = other.astype(jnp.bfloat16)


def add_kernel(own_ref, back_ref, after_ref, out_ref):
    out_ref[...] = sum_of(own_ref, back_ref)


def last_pair_kernel(own_ref, back_ref, out_ref):
    total = own_ref[...].astype(jnp.float32) + back_ref[...].astype(jnp.float32)
    out_ref[...] = total.astype(jnp.bfloat16)


def block_of(value, width):
    whole, index = value
    rows = whole.shape[-2]
    lead = len(index)
    return pl.BlockSpec((None,) * lead + (rows, width), lambda step: index + (0, step))


def all_of(value):
    whole, index = value
    lead = len(index)
    return pl.BlockSpec((None,) * lead + whole.shape[-2:], lambda step: index + (0, 0))


def lean_pack(where, capacity, values, gain, ids):
    rows, width = values[0][0].shape[-2:]
    room = EXPERTS * capacity
    block = split(width, 2)
    packed = pl.BlockSpec((room, block), lambda step: (0, step))
    summed = len(values) > 1
    whole = pl.BlockSpec((rows, width), lambda step: (0, 0))
    return pl.pallas_call(
        functools.partial(sum_pack_kernel if summed else lean_pack_kernel, where, capacity),
        grid=(width // block,),
        out_shape=(array(rows, width), array(room, width)) if summed else array(room, width),
        in_specs=[all_of(value) for value in values] + [all_of(gain), VMEM],
        out_specs=(whole, packed) if summed else packed,
        scratch_shapes=(
            pltpu.VMEM((rows, width), jnp.bfloat16),
            pltpu.VMEM((room, rows), jnp.bfloat16),
        ),
        compiler_params=params(),
    )(*[value[0] for value in values], gain[0], ids)


def wide_pack(where, capacity, values, gain, ids, other_ids, after, flag=None):
    rows, width = values[0][0].shape[-2:]
    room = EXPERTS * 2 * capacity
    block = split(width, 2)
    packed = pl.BlockSpec((room, block), lambda step: (0, step))
    whole = pl.BlockSpec((rows, width), lambda step: (0, 0))
    picks = flag is not None
    scratch = (
        pltpu.VMEM((2 * rows, width), jnp.bfloat16),
        pltpu.VMEM((room, 2 * rows), jnp.bfloat16),
    )
    return pl.pallas_call(
        functools.partial(either_pack_kernel if picks else wide_pack_kernel, where, capacity),
        grid=(width // block,),
        out_shape=(array(rows, width), array(room, width)) if picks else array(room, width),
        in_specs=[SMEM] * picks
        + [all_of(value) for value in values]
        + [all_of(gain), VMEM, VMEM, ANY],
        out_specs=(whole, packed) if picks else packed,
        scratch_shapes=scratch + (pltpu.VMEM((rows, width), jnp.bfloat16),) * picks,
        compiler_params=params(),
    )(*[flag] * picks, *[value[0] for value in values], gain[0], ids, other_ids, after)


def combine(where, capacity, value, rows, ids, weights, last=None):
    tokens = ids.shape[-1]
    room, width = rows.shape
    block = split(width, 2)
    specs = [block_of(value, block), block_of((rows, ()), block), VMEM, VMEM]
    args = [value[0], rows, ids, weights]
    scratch = (pltpu.VMEM((2 * tokens, room), jnp.bfloat16),)
    if last is None:
        return pl.pallas_call(
            functools.partial(combine_kernel, where, capacity),
            grid=(width // block,),
            out_shape=array(tokens, width),
            in_specs=specs,
            out_specs=pl.BlockSpec((tokens, block), lambda step: (0, step)),
            scratch_shapes=scratch,
            compiler_params=params(),
        )(*args)
    flag, instead, held, leg = last
    return pl.pallas_call(
        functools.partial(last_combine_kernel, where, capacity),
        grid=(width // block,),
        out_shape=array(*held.shape),
        in_specs=[SMEM] + specs + [block_of((instead, ()), block), ANY],
        out_specs=pl.BlockSpec((None, None, tokens, block), lambda step: (leg, 0, 0, step)),
        scratch_shapes=scratch,
        input_output_aliases={6: 0},
        compiler_params=params(),
    )(flag, *args, instead, held)


def pair_combine(
    where, capacity, value, rows, ids, weights, other_ids, other_weights, kind=jnp.bfloat16
):
    tokens = ids.shape[-1]
    room, width = rows.shape
    block = split(width, 2)
    part = pl.BlockSpec((tokens, block), lambda step: (0, step))
    return pl.pallas_call(
        functools.partial(pair_combine_kernel, where, capacity),
        grid=(width // block,),
        out_shape=(array(tokens, width, dtype=kind), array(tokens, width)),
        in_specs=[block_of(value, block), block_of((rows, ()), block)] + [VMEM] * 4,
        out_specs=(part, part),
        scratch_shapes=(pltpu.VMEM((4 * tokens, room), jnp.bfloat16),),
        compiler_params=params(),
    )(value[0], rows, ids, weights, other_ids, other_weights)


def last_pair(own, back, leg):
    tokens, width = own.shape
    block = split(width, 2)
    part = pl.BlockSpec((tokens, block), lambda step: (0, step))
    return pl.pallas_call(
        last_pair_kernel,
        grid=(width // block,),
        out_shape=array(2, 1, tokens, width),
        in_specs=[part, part],
        out_specs=pl.BlockSpec((None, None, tokens, block), lambda step: (leg, 0, 0, step)),
        compiler_params=params(),
    )(own, back)


def add(own, back, after):
    rows, width = own.shape
    half = pl.BlockSpec((rows // 2, width), lambda step: (step, 0))
    return pl.pallas_call(
        add_kernel,
        grid=(2,),
        out_shape=array(*own.shape),
        in_specs=[half, half, ANY],
        out_specs=half,
        compiler_params=params(),
    )(own, back, after)


def pieces(width, first):
    unit = width // 7
    if width % 7 or unit % 128:
        return [slice(0, width)]
    sizes = [unit, 2 * unit, 2 * unit, 2 * unit]
    if not first:
        sizes.reverse()
    starts = [sum(sizes[:number]) for number in range(4)]
    return [slice(start, start + size) for start, size in zip(starts, sizes)]


def expert_pass(rows, leg, gate_cols, up_cols, down_rows, after):
    count, width = rows.shape
    hidden = gate_cols.shape[-1]
    deep, wide = pieces(width, True), pieces(width, False)
    arrivals = pltpu.SemaphoreType.DMA((len(deep),))
    return pl.pallas_call(
        functools.partial(expert_kernel, leg, deep, wide),
        out_shape=array(count, width),
        in_specs=[ANY] * 5,
        out_specs=ANY,
        scratch_shapes=(
            pltpu.VMEM((count, width), jnp.bfloat16),
            pltpu.VMEM((width, hidden), jnp.bfloat16),
            pltpu.VMEM((width, hidden), jnp.bfloat16),
            pltpu.VMEM((hidden, width), jnp.bfloat16),
            pltpu.VMEM((count, width), jnp.bfloat16),
            pltpu.VMEM((count, hidden), jnp.float32),
            pltpu.VMEM((count, hidden), jnp.float32),
            pltpu.VMEM((count, hidden), jnp.bfloat16),
            arrivals,
            arrivals,
            arrivals,
            arrivals,
            arrivals,
        ),
        compiler_params=params(),
        cost_estimate=pl.CostEstimate(
            flops=6 * count * width * hidden,
            bytes_accessed=2 * (2 * count * width + 3 * width * hidden),
            transcendentals=count * hidden,
        ),
    )(rows, gate_cols, up_cols, down_rows, after)


def on_device(in_flight, routes, gate_weights, norm_gain, w_gate, w_up, w_down):
    section_count = lax.axis_size("pp")
    section_pos = lax.axis_index("pp")
    tokens, top_count = routes.shape[-2:]
    capacity = tokens * top_count * 5 // (4 * EXPERTS)
    down = (in_flight, (0, 0))
    up = (in_flight, (1, 0))
    down_other = other_half(in_flight[0, 0])
    ids = jnp.swapaxes(routes[:, :, 0], -1, -2)
    weights = jnp.swapaxes(gate_weights[:, :, 0], -1, -2)
    other_ids = other_half(ids)
    other_weights = other_half(weights)
    gains = norm_gain[:, :, None]

    def experts(rows, leg, after):
        return expert_pass(rows, leg, w_gate, w_up, w_down, after)

    def worked(tick, wide, wide_value, wide_packed, lean, lean_own, kind):
        wide_rows = within_column(wide_packed)
        lean_other = other_half(lean_own)
        part_own = experts(lean_own, lean, ids)
        wide_out = experts(wide_rows, wide, part_own)
        part_back = other_half(experts(lean_other, lean, wide_out))
        wide_back = within_column(wide_out)
        own, other = pair_combine(
            (tick, wide),
            capacity,
            wide_value,
            wide_back,
            ids,
            weights,
            other_ids,
            other_weights,
            kind,
        )
        return own, other, within_column(add(part_own, part_back, other))

    lean_own = within_column(lean_pack((0, 1), capacity, [up], (gains, (1, 0)), ids))
    wide_packed = wide_pack(
        (0, 0),
        capacity,
        [down, (down_other, ())],
        (gains, (0, 0)),
        ids,
        other_ids,
        other_weights,
    )
    own, other, lean_back = worked(0, 0, down, wide_packed, 1, lean_own, jnp.bfloat16)
    own_down, other_down = moved(own, 1, 0), moved(other, 1, 1)
    own_turned, other_turned = moved(own, 0, 1), moved(other, 0, 1)
    first_up = combine((0, 1), capacity, up, lean_back, ids, weights)
    descending, lean_packed = lean_pack(
        (1, 0), capacity, [(own_down, ()), (other_down, ())], (gains, (0, 0)), ids
    )
    lean_own = within_column(lean_packed)
    folds = (section_pos == section_count - 1).astype(jnp.int32).reshape(1)
    turned, wide_packed = wide_pack(
        (1, 1),
        capacity,
        [
            (value, ())
            for value in (
                moved(first_up, -1, 0),
                moved(first_up, -1, 1),
                own,
                other_turned,
                own_turned,
                other,
            )
        ],
        (gains, (1, 0)),
        ids,
        other_ids,
        other_weights,
        folds,
    )
    own, other, lean_back = worked(1, 1, (turned, ()), wide_packed, 0, lean_own, jnp.float32)
    result = last_pair(own, other_half(other), 1)
    starts = (section_pos == 0).astype(jnp.int32).reshape(1)
    return combine(
        (1, 0), capacity, (descending, ()), lean_back, ids, weights, (starts, first_up, result, 0)
    )


def solution(mesh):
    placed = (
        P(None, "pp", "ep", None),
        P(None, None, "pp", "ep", None),
        P(None, None, "pp", "ep", None),
        P(None, "pp", None),
        P(None, "pp", None, "ep"),
        P(None, "pp", None, "ep"),
        P(None, "pp", "ep", None),
    )
    return jax.shard_map(
        on_device, mesh=mesh, in_specs=placed, out_specs=P(None, "pp", "ep", None), check_vma=False
    )
```

```python
import functools

import jax
import jax.numpy as jnp
from jax import lax
from jax.experimental import pallas as pl
from jax.experimental.pallas import tpu as pltpu
from jax.sharding import PartitionSpec as P

SIDE = 4
COLUMNS = (
    [SIDE * z + x for z in range(SIDE) for x in (0, 3)],
    [SIDE * z + x for z in range(SIDE) for x in (1, 2)],
)
EXPERTS = 2 * SIDE
ROOM = 62 * 2**20
WORK = 5 * 10**10
VMEM = pl.BlockSpec(memory_space=pltpu.VMEM)
SMEM = pl.BlockSpec(memory_space=pltpu.SMEM)
ANY = pl.BlockSpec(memory_space=pl.ANY)


def moved(value, steps, crossed):
    sections, places = lax.axis_size("pp"), lax.axis_size("ep")
    if steps == 0:
        sources = [sections - 1]
    else:
        sources = [section for section in range(sections) if 0 <= section + steps < sections]
    pairs = [
        (section * places + place, (section + steps) * places + (place ^ crossed))
        for section in sources
        for place in range(places)
    ]
    return lax.ppermute(value, ("pp", "ep"), pairs)


def other_half(value):
    return lax.ppermute(value, "ep", [(place, place ^ 1) for place in range(lax.axis_size("ep"))])


def within_column(rows):
    shape = rows.shape
    received = lax.all_to_all(
        rows.reshape(EXPERTS, shape[0] // EXPERTS, shape[1]),
        "ep",
        split_axis=0,
        concat_axis=0,
        tiled=True,
        axis_index_groups=COLUMNS,
    )
    return received.reshape(shape)


def iota(shape, dim):
    return lax.broadcasted_iota(jnp.int32, shape, dim)


def dot(left, right):
    return jnp.dot(left, right, preferred_element_type=jnp.float32)


def array(*shape, dtype=jnp.bfloat16):
    return jax.ShapeDtypeStruct(shape, dtype)


def split(width, parts):
    return width // parts if width % (128 * parts) == 0 else width


def params():
    return pltpu.CompilerParams(vmem_limit_bytes=ROOM)


def normalise(value, gain):
    widened = value.astype(jnp.float32)
    scale = lax.rsqrt(jnp.mean(widened * widened, axis=-1, keepdims=True) + 1e-06)
    return (widened * scale * gain).astype(jnp.bfloat16)


def slots(ids):
    tokens = ids.shape[1]
    expert = iota((EXPERTS, tokens), 0)
    named = (ids[0:1] == expert) | (ids[1:2] == expert)
    before = (iota((tokens, tokens), 0) < iota((tokens, tokens), 1)).astype(jnp.bfloat16)
    earlier = dot(jnp.where(named, 1.0, 0.0).astype(jnp.bfloat16), before)
    return jnp.where(named, earlier, -1.0)


def slot_matrix(ids, capacity, first, room, weights=None):
    tokens = ids.shape[1]
    slot = slots(ids)
    place = iota((EXPERTS, room, tokens), 1).astype(jnp.float32) - float(first)
    if weights is None:
        value = 1.0
    else:
        expert = iota((EXPERTS, tokens), 0)
        value = jnp.where(ids[0:1] == expert, weights[0:1], 0.0) + jnp.where(
            ids[1:2] == expert, weights[1:2], 0.0
        )
        value = value[:, None, :]
    chosen = (slot[:, None, :] == place) & (place >= 0.0)
    return jnp.where(chosen, value, 0.0).reshape(EXPERTS * room, tokens)


def two_terms(matrix):
    high = matrix.astype(jnp.bfloat16)
    return high, (matrix - high.astype(jnp.float32)).astype(jnp.bfloat16)


def across(matrix):
    rows, tokens = matrix.shape
    extra = -rows % 128
    if extra:
        matrix = jnp.concatenate([matrix, jnp.zeros((extra, tokens), matrix.dtype)], axis=0)
    return matrix.T[:, :rows]


def wide_matrix(ids, other_ids, capacity):
    room = 2 * capacity
    own = slot_matrix(ids, capacity, 0, room)
    other = slot_matrix(other_ids, capacity, capacity, room)
    return jnp.concatenate([own, other], axis=1).astype(jnp.bfloat16)


def lean_weight_matrix(ids, weights, capacity):
    return jnp.concatenate(
        two_terms(across(slot_matrix(ids, capacity, 0, capacity, weights))), axis=0
    )


def wide_weight_matrix(ids, weights, other_ids, other_weights, capacity):
    room = 2 * capacity
    own = two_terms(across(slot_matrix(ids, capacity, 0, room, weights)))
    other = two_terms(across(slot_matrix(other_ids, capacity, capacity, room, other_weights)))
    return jnp.concatenate(own + other, axis=0)


def plan_kernel(
    capacity,
    ids_ref,
    weights_ref,
    other_ids_ref,
    other_weights_ref,
    after_ref,
    wide_first,
    lean_first,
    lean_rows,
    wide_rows,
    wide_second,
    lean_second,
):
    def wide(tick):
        place = (tick, tick)
        return wide_weight_matrix(
            ids_ref[place],
            weights_ref[place],
            other_ids_ref[place],
            other_weights_ref[place],
            capacity,
        )

    def lean(tick):
        place = (tick, 1 - tick)
        return lean_weight_matrix(ids_ref[place], weights_ref[place], capacity)

    wide_first[...], lean_first[...] = wide(0), lean(0)
    wide_second[...], lean_second[...] = wide(1), lean(1)
    lean_rows[...] = slot_matrix(ids_ref[1, 0], capacity, 0, capacity).astype(jnp.bfloat16)
    wide_rows[...] = wide_matrix(ids_ref[1, 1], other_ids_ref[1, 1], capacity)


def spread(matrix_ref, normed_ref, out_ref):
    width = out_ref.shape[1]
    cols = pl.ds(pl.multiple_of(pl.program_id(0) * width, 128), width)
    out_ref[...] = dot(matrix_ref[...], normed_ref[:, cols]).astype(jnp.bfloat16)


def sum_of(first_ref, second_ref):
    total = first_ref[...].astype(jnp.float32) + second_ref[...].astype(jnp.float32)
    return total.astype(jnp.bfloat16)


def lean_pack_kernel(where, capacity, value_ref, gain_ref, ids_ref, out_ref, normed_ref, matrix_ref):
    @pl.when(pl.program_id(0) == 0)
    def _():
        normed_ref[...] = normalise(value_ref[...], gain_ref[...])
        matrix_ref[...] = slot_matrix(ids_ref[where], capacity, 0, capacity).astype(jnp.bfloat16)

    spread(matrix_ref, normed_ref, out_ref)


def sum_pack_kernel(
    first_ref,
    second_ref,
    gain_ref,
    matrix_ref,
    after_ref,
    own_turned_ref,
    other_turned_ref,
    value_ref,
    out_ref,
    normed_ref,
):
    @pl.when(pl.program_id(0) == 0)
    def _():
        value_ref[...] = sum_of(first_ref, second_ref)
        normed_ref[...] = normalise(value_ref[...], gain_ref[...])

    spread(matrix_ref, normed_ref, out_ref)


def wide_pack_kernel(
    where,
    capacity,
    own_ref,
    other_ref,
    gain_ref,
    ids_ref,
    other_ids_ref,
    after_ref,
    out_ref,
    normed_ref,
    matrix_ref,
):
    @pl.when(pl.program_id(0) == 0)
    def _():
        tokens = own_ref.shape[0]
        normed_ref[:tokens] = normalise(own_ref[...], gain_ref[...])
        normed_ref[tokens:] = normalise(other_ref[...], gain_ref[...])
        matrix_ref[...] = wide_matrix(ids_ref[where], other_ids_ref[where], capacity)

    spread(matrix_ref, normed_ref, out_ref)


def either_pack_kernel(
    flag_ref,
    own_ref,
    other_ref,
    own_first_ref,
    own_second_ref,
    other_first_ref,
    other_second_ref,
    gain_ref,
    matrix_ref,
    value_ref,
    out_ref,
    normed_ref,
):
    first = pl.program_id(0) == 0
    tokens = own_ref.shape[0]

    @pl.when(first & (flag_ref[0] == 0))
    def _():
        value_ref[...] = own_ref[...]
        normed_ref[:tokens] = normalise(own_ref[...], gain_ref[...])
        normed_ref[tokens:] = normalise(other_ref[...], gain_ref[...])

    @pl.when(first & (flag_ref[0] != 0))
    def _():
        value_ref[...] = sum_of(own_first_ref, own_second_ref)
        normed_ref[:tokens] = normalise(value_ref[...], gain_ref[...])
        normed_ref[tokens:] = normalise(sum_of(other_first_ref, other_second_ref), gain_ref[...])

    spread(matrix_ref, normed_ref, out_ref)


def expert_kernel(
    leg,
    deep,
    wide,
    rows_ref,
    gate_ref,
    up_ref,
    down_ref,
    after_ref,
    out_ref,
    rows,
    gate_cols,
    up_cols,
    down_rows,
    results,
    gate_sum,
    up_sum,
    active,
    rows_in,
    gate_in,
    up_in,
    down_in,
    results_out,
):
    arriving = []
    for number, cols in enumerate(deep):
        arriving.append(
            (
                pltpu.make_async_copy(rows_ref.at[:, cols], rows.at[:, cols], rows_in.at[number]),
                pltpu.make_async_copy(
                    gate_ref.at[leg, 0, cols], gate_cols.at[cols], gate_in.at[number]
                ),
                pltpu.make_async_copy(up_ref.at[leg, 0, cols], up_cols.at[cols], up_in.at[number]),
            )
        )
    for number, cols in enumerate(wide):
        arriving.append(
            (
                pltpu.make_async_copy(
                    down_ref.at[leg, 0, :, cols], down_rows.at[:, cols], down_in.at[number]
                ),
            )
        )
    for copies in arriving:
        for copy in copies:
            copy.start()
    for number, cols in enumerate(deep):
        for copy in arriving[number]:
            copy.wait()
        gate = dot(rows[:, cols], gate_cols[cols])
        up = dot(rows[:, cols], up_cols[cols])
        if number > 0:
            gate = gate + gate_sum[...]
            up = up + up_sum[...]
        if number < len(deep) - 1:
            gate_sum[...] = gate
            up_sum[...] = up
        else:
            active[...] = (jax.nn.silu(gate) * up).astype(jnp.bfloat16)
    leaving = []
    for number, cols in enumerate(wide):
        for copy in arriving[len(deep) + number]:
            copy.wait()
        results[:, cols] = dot(active[...], down_rows[:, cols]).astype(jnp.bfloat16)
        copy = pltpu.make_async_copy(
            results.at[:, cols], out_ref.at[:, cols], results_out.at[number]
        )
        copy.start()
        leaving.append(copy)
    for copy in leaving:
        copy.wait()


def combine_kernel(value_ref, rows_ref, matrix_ref, out_ref):
    tokens = out_ref.shape[0]
    terms = dot(matrix_ref[...], rows_ref[...])
    mixture = terms[:tokens] + terms[tokens:]
    out_ref[...] = (value_ref[...].astype(jnp.float32) + mixture).astype(jnp.bfloat16)


def last_combine_kernel(
    flag_ref, value_ref, rows_ref, matrix_ref, instead_ref, held_ref, out_ref
):
    combine_kernel(value_ref, rows_ref, matrix_ref, out_ref)

    @pl.when(flag_ref[0] != 0)
    def _():
        out_ref[...] = instead_ref[...]


def pair_combine_kernel(value_ref, rows_ref, matrix_ref, after_ref, own_ref, other_ref):
    tokens = own_ref.shape[0]
    terms = dot(matrix_ref[...], rows_ref[...])
    own = value_ref[...].astype(jnp.float32) + terms[:tokens] + terms[tokens : 2 * tokens]
    own_ref[...] = own.astype(own_ref.dtype)
    other = terms[2 * tokens : 3 * tokens] + terms[3 * tokens :]
    other_ref[...] = other.astype(jnp.bfloat16)


def add_kernel(own_ref, back_ref, after_ref, out_ref):
    out_ref[...] = sum_of(own_ref, back_ref)


def last_pair_kernel(own_ref, back_ref, out_ref):
    total = own_ref[...].astype(jnp.float32) + back_ref[...].astype(jnp.float32)
    out_ref[...] = total.astype(jnp.bfloat16)


def block_of(value, width):
    whole, index = value
    rows = whole.shape[-2]
    lead = len(index)
    return pl.BlockSpec((None,) * lead + (rows, width), lambda step: index + (0, step))


def all_of(value):
    whole, index = value
    lead = len(index)
    return pl.BlockSpec((None,) * lead + whole.shape[-2:], lambda step: index + (0, 0))


def plan(capacity, ids, weights, other_ids, other_weights, after):
    tokens = ids.shape[-1]
    lean, wide = EXPERTS * capacity, EXPERTS * 2 * capacity
    shapes = (
        (4 * tokens, wide),
        (2 * tokens, lean),
        (lean, tokens),
        (wide, 2 * tokens),
        (4 * tokens, wide),
        (2 * tokens, lean),
    )
    return pl.pallas_call(
        functools.partial(plan_kernel, capacity),
        grid=(1,),
        out_shape=[array(*shape) for shape in shapes],
        in_specs=[VMEM] * 4 + [ANY],
        out_specs=[pl.BlockSpec(shape, lambda step: (0, 0)) for shape in shapes],
        compiler_params=params(),
    )(ids, weights, other_ids, other_weights, after)


def pack(kernel, values, room, gain, others, scratch=(), flag=None, summed=False, work=0):
    rows, width = values[0][0].shape[-2:]
    block = split(width, 2)
    packed = pl.BlockSpec((room, block), lambda step: (0, step))
    whole = pl.BlockSpec((rows, width), lambda step: (0, 0))
    picks = flag is not None
    return pl.pallas_call(
        kernel,
        grid=(width // block,),
        out_shape=(array(rows, width), array(room, width)) if summed else array(room, width),
        in_specs=[SMEM] * picks
        + [all_of(value) for value in values]
        + [all_of(gain)]
        + [spec for _, spec in others],
        out_specs=(whole, packed) if summed else packed,
        scratch_shapes=scratch,
        compiler_params=params(),
        cost_estimate=pl.CostEstimate(flops=work, bytes_accessed=0, transcendentals=0)
        if work
        else None,
    )(*[flag] * picks, *[value[0] for value in values], gain[0], *[other for other, _ in others])


def combine(value, rows, matrix, last=None):
    width = rows.shape[1]
    tokens = matrix.shape[0] // 2
    block = split(width, 2)
    specs = [block_of(value, block), block_of((rows, ()), block), VMEM]
    args = [value[0], rows, matrix]
    if last is None:
        return pl.pallas_call(
            combine_kernel,
            grid=(width // block,),
            out_shape=array(tokens, width),
            in_specs=specs,
            out_specs=pl.BlockSpec((tokens, block), lambda step: (0, step)),
            compiler_params=params(),
        )(*args)
    flag, instead, held, leg = last
    return pl.pallas_call(
        last_combine_kernel,
        grid=(width // block,),
        out_shape=array(*held.shape),
        in_specs=[SMEM] + specs + [block_of((instead, ()), block), ANY],
        out_specs=pl.BlockSpec((None, None, tokens, block), lambda step: (leg, 0, 0, step)),
        input_output_aliases={5: 0},
        compiler_params=params(),
    )(flag, *args, instead, held)


def pair_combine(value, rows, matrix, after, kind):
    width = rows.shape[1]
    tokens = matrix.shape[0] // 4
    block = split(width, 2)
    part = pl.BlockSpec((tokens, block), lambda step: (0, step))
    return pl.pallas_call(
        pair_combine_kernel,
        grid=(width // block,),
        out_shape=(array(tokens, width, dtype=kind), array(tokens, width)),
        in_specs=[block_of(value, block), block_of((rows, ()), block), VMEM, ANY],
        out_specs=(part, part),
        compiler_params=params(),
    )(value[0], rows, matrix, after)


def last_pair(own, back, leg):
    tokens, width = own.shape
    block = split(width, 2)
    part = pl.BlockSpec((tokens, block), lambda step: (0, step))
    return pl.pallas_call(
        last_pair_kernel,
        grid=(width // block,),
        out_shape=array(2, 1, tokens, width),
        in_specs=[part, part],
        out_specs=pl.BlockSpec((None, None, tokens, block), lambda step: (leg, 0, 0, step)),
        compiler_params=params(),
    )(own, back)


def add(own, back, after):
    rows, width = own.shape
    half = pl.BlockSpec((rows // 2, width), lambda step: (step, 0))
    return pl.pallas_call(
        add_kernel,
        grid=(2,),
        out_shape=array(*own.shape),
        in_specs=[half, half, ANY],
        out_specs=half,
        compiler_params=params(),
    )(own, back, after)


def pieces(width, sizes):
    unit = width // 7
    if width % 7 or unit % 128:
        return [slice(0, width)]
    sizes = [size * unit for size in sizes]
    starts = [sum(sizes[:number]) for number in range(len(sizes))]
    return [slice(start, start + size) for start, size in zip(starts, sizes)]


def expert_pass(rows, leg, gate_cols, up_cols, down_rows, after):
    count, width = rows.shape
    hidden = gate_cols.shape[-1]
    deep = pieces(width, (1, 2, 2, 2) if count > 512 else (1,) * 7)
    wide = pieces(width, (2, 2, 2, 1))
    arrivals = pltpu.SemaphoreType.DMA((len(deep),))
    return pl.pallas_call(
        functools.partial(expert_kernel, leg, deep, wide),
        out_shape=array(count, width),
        in_specs=[ANY] * 5,
        out_specs=ANY,
        scratch_shapes=(
            pltpu.VMEM((count, width), jnp.bfloat16),
            pltpu.VMEM((width, hidden), jnp.bfloat16),
            pltpu.VMEM((width, hidden), jnp.bfloat16),
            pltpu.VMEM((hidden, width), jnp.bfloat16),
            pltpu.VMEM((count, width), jnp.bfloat16),
            pltpu.VMEM((count, hidden), jnp.float32),
            pltpu.VMEM((count, hidden), jnp.float32),
            pltpu.VMEM((count, hidden), jnp.bfloat16),
            arrivals,
            arrivals,
            arrivals,
            arrivals,
            arrivals,
        ),
        compiler_params=params(),
        cost_estimate=pl.CostEstimate(
            flops=6 * count * width * hidden,
            bytes_accessed=2 * (2 * count * width + 3 * width * hidden),
            transcendentals=count * hidden,
        ),
    )(rows, gate_cols, up_cols, down_rows, after)


def on_device(in_flight, routes, gate_weights, norm_gain, w_gate, w_up, w_down):
    section_count = lax.axis_size("pp")
    section_pos = lax.axis_index("pp")
    tokens, top_count = routes.shape[-2:]
    width = in_flight.shape[-1]
    capacity = tokens * top_count * 5 // (4 * EXPERTS)
    down = (in_flight, (0, 0))
    up = (in_flight, (1, 0))
    down_other = other_half(in_flight[0, 0])
    ids = jnp.swapaxes(routes[:, :, 0], -1, -2)
    weights = jnp.swapaxes(gate_weights[:, :, 0], -1, -2)
    other_ids = other_half(ids)
    other_weights = other_half(weights)
    gains = norm_gain[:, :, None]

    def experts(rows, leg, after):
        return expert_pass(rows, leg, w_gate, w_up, w_down, after)

    def worked(wide, wide_packed, lean, lean_own):
        wide_rows = within_column(wide_packed)
        lean_other = other_half(lean_own)
        part_own = experts(lean_own, lean, ids)
        wide_out = experts(wide_rows, wide, part_own)
        part_back = other_half(experts(lean_other, lean, wide_out))
        return within_column(wide_out), part_own, part_back

    lean_rows, wide_rows = EXPERTS * capacity, EXPERTS * 2 * capacity
    packed = pack(
        functools.partial(lean_pack_kernel, (0, 1), capacity),
        [up],
        lean_rows,
        (gains, (1, 0)),
        [(ids, VMEM)],
        (pltpu.VMEM((tokens, width), jnp.bfloat16), pltpu.VMEM((lean_rows, tokens), jnp.bfloat16)),
    )
    lean_own = within_column(packed)
    packed = pack(
        functools.partial(wide_pack_kernel, (0, 0), capacity),
        [down, (down_other, ())],
        wide_rows,
        (gains, (0, 0)),
        [(ids, VMEM), (other_ids, VMEM), (other_weights, ANY)],
        (
            pltpu.VMEM((2 * tokens, width), jnp.bfloat16),
            pltpu.VMEM((wide_rows, 2 * tokens), jnp.bfloat16),
        ),
    )
    wide_back, part_own, part_back = worked(0, packed, 1, lean_own)
    plans = plan(capacity, ids, weights, other_ids, other_weights, part_own)
    wide_first, lean_first, lean_matrix, wide_matrix_next, wide_second, lean_second = plans
    lean_out = add(part_own, part_back, wide_first)
    lean_back = within_column(lean_out)
    own, other = pair_combine(down, wide_back, wide_first, lean_out, jnp.bfloat16)
    own_down, other_down = moved(own, 1, 0), moved(other, 1, 1)
    own_turned, other_turned = moved(own, 0, 1), moved(other, 0, 1)
    first_up = combine(up, lean_back, lean_first)
    descending, packed = pack(
        sum_pack_kernel,
        [(own_down, ()), (other_down, ())],
        lean_rows,
        (gains, (0, 0)),
        [(lean_matrix, VMEM), (first_up, ANY), (own_turned, ANY), (other_turned, ANY)],
        (pltpu.VMEM((tokens, width), jnp.bfloat16),),
        summed=True,
    )
    lean_own = within_column(packed)
    folds = (section_pos == section_count - 1).astype(jnp.int32).reshape(1)
    turned, packed = pack(
        either_pack_kernel,
        [
            (value, ())
            for value in (
                moved(first_up, -1, 0),
                moved(first_up, -1, 1),
                own,
                other_turned,
                own_turned,
                other,
            )
        ],
        wide_rows,
        (gains, (1, 0)),
        [(wide_matrix_next, VMEM)],
        (pltpu.VMEM((2 * tokens, width), jnp.bfloat16),),
        flag=folds,
        summed=True,
        work=WORK,
    )
    wide_back, part_own, part_back = worked(1, packed, 0, lean_own)
    lean_out = add(part_own, part_back, wide_second)
    lean_back = within_column(lean_out)
    own, other = pair_combine((turned, ()), wide_back, wide_second, lean_out, jnp.float32)
    result = last_pair(own, other_half(other), 1)
    starts = (section_pos == 0).astype(jnp.int32).reshape(1)
    return combine((descending, ()), lean_back, lean_second, (starts, first_up, result, 0))


def solution(mesh):
    placed = (
        P(None, "pp", "ep", None),
        P(None, None, "pp", "ep", None),
        P(None, None, "pp", "ep", None),
        P(None, "pp", None),
        P(None, "pp", None, "ep"),
        P(None, "pp", None, "ep"),
        P(None, "pp", "ep", None),
    )
    return jax.shard_map(
        on_device, mesh=mesh, in_specs=placed, out_specs=P(None, "pp", "ep", None), check_vma=False
    )
```

```python
import functools

import jax
import jax.numpy as jnp
from jax import lax
from jax.experimental import pallas as pl
from jax.experimental.pallas import tpu as pltpu
from jax.sharding import PartitionSpec as P

SIDE = 4
COLUMNS = (
    [SIDE * z + x for z in range(SIDE) for x in (0, 3)],
    [SIDE * z + x for z in range(SIDE) for x in (1, 2)],
)
EXPERTS = 2 * SIDE
ROOM = 62 * 2**20
WORK = 5 * 10**10
VMEM = pl.BlockSpec(memory_space=pltpu.VMEM)
SMEM = pl.BlockSpec(memory_space=pltpu.SMEM)
ANY = pl.BlockSpec(memory_space=pl.ANY)


def moved(value, steps, crossed):
    sections, places = lax.axis_size("pp"), lax.axis_size("ep")
    if steps == 0:
        sources = [sections - 1]
    else:
        sources = [section for section in range(sections) if 0 <= section + steps < sections]
    pairs = [
        (section * places + place, (section + steps) * places + (place ^ crossed))
        for section in sources
        for place in range(places)
    ]
    return lax.ppermute(value, ("pp", "ep"), pairs)


def other_half(value):
    return lax.ppermute(value, "ep", [(place, place ^ 1) for place in range(lax.axis_size("ep"))])


def within_column(rows):
    shape = rows.shape
    received = lax.all_to_all(
        rows.reshape(EXPERTS, shape[0] // EXPERTS, shape[1]),
        "ep",
        split_axis=0,
        concat_axis=0,
        tiled=True,
        axis_index_groups=COLUMNS,
    )
    return received.reshape(shape)


def iota(shape, dim):
    return lax.broadcasted_iota(jnp.int32, shape, dim)


def dot(left, right):
    return jnp.dot(left, right, preferred_element_type=jnp.float32)


def array(*shape, dtype=jnp.bfloat16):
    return jax.ShapeDtypeStruct(shape, dtype)


def split(width, parts):
    return width // parts if width % (128 * parts) == 0 else width


def params():
    return pltpu.CompilerParams(vmem_limit_bytes=ROOM)


def normalise(value, gain):
    widened = value.astype(jnp.float32)
    scale = lax.rsqrt(jnp.mean(widened * widened, axis=-1, keepdims=True) + 1e-06)
    return (widened * scale * gain).astype(jnp.bfloat16)


def slots(ids):
    tokens = ids.shape[1]
    expert = iota((EXPERTS, tokens), 0)
    named = (ids[0:1] == expert) | (ids[1:2] == expert)
    before = (iota((tokens, tokens), 0) < iota((tokens, tokens), 1)).astype(jnp.bfloat16)
    earlier = dot(jnp.where(named, 1.0, 0.0).astype(jnp.bfloat16), before)
    return jnp.where(named, earlier, -1.0)


def slot_matrix(ids, capacity, first, room, weights=None):
    tokens = ids.shape[1]
    slot = slots(ids)
    place = iota((EXPERTS, room, tokens), 1).astype(jnp.float32) - float(first)
    if weights is None:
        value = 1.0
    else:
        expert = iota((EXPERTS, tokens), 0)
        value = jnp.where(ids[0:1] == expert, weights[0:1], 0.0) + jnp.where(
            ids[1:2] == expert, weights[1:2], 0.0
        )
        value = value[:, None, :]
    chosen = (slot[:, None, :] == place) & (place >= 0.0)
    return jnp.where(chosen, value, 0.0).reshape(EXPERTS * room, tokens)


def two_terms(matrix):
    high = matrix.astype(jnp.bfloat16)
    return high, (matrix - high.astype(jnp.float32)).astype(jnp.bfloat16)


def across(matrix):
    rows, tokens = matrix.shape
    extra = -rows % 128
    if extra:
        matrix = jnp.concatenate([matrix, jnp.zeros((extra, tokens), matrix.dtype)], axis=0)
    return matrix.T[:, :rows]


def wide_matrix(ids, other_ids, capacity):
    room = 2 * capacity
    own = slot_matrix(ids, capacity, 0, room)
    other = slot_matrix(other_ids, capacity, capacity, room)
    return jnp.concatenate([own, other], axis=1).astype(jnp.bfloat16)


def lean_weight_matrix(ids, weights, capacity):
    return jnp.concatenate(
        two_terms(across(slot_matrix(ids, capacity, 0, capacity, weights))), axis=0
    )


def wide_weight_matrix(ids, weights, other_ids, other_weights, capacity):
    room = 2 * capacity
    own = two_terms(across(slot_matrix(ids, capacity, 0, room, weights)))
    other = two_terms(across(slot_matrix(other_ids, capacity, capacity, room, other_weights)))
    return jnp.concatenate(own + other, axis=0)


def plan_kernel(
    capacity,
    ids_ref,
    weights_ref,
    other_ids_ref,
    other_weights_ref,
    after_ref,
    wide_first,
    lean_first,
    lean_rows,
    wide_rows,
    wide_second,
    lean_second,
):
    def wide(tick):
        place = (tick, tick)
        return wide_weight_matrix(
            ids_ref[place],
            weights_ref[place],
            other_ids_ref[place],
            other_weights_ref[place],
            capacity,
        )

    def lean(tick):
        place = (tick, 1 - tick)
        return lean_weight_matrix(ids_ref[place], weights_ref[place], capacity)

    wide_first[...], lean_first[...] = wide(0), lean(0)
    wide_second[...], lean_second[...] = wide(1), lean(1)
    lean_rows[...] = slot_matrix(ids_ref[1, 0], capacity, 0, capacity).astype(jnp.bfloat16)
    wide_rows[...] = wide_matrix(ids_ref[1, 1], other_ids_ref[1, 1], capacity)


def spread(matrix_ref, normed_ref, out_ref):
    width = out_ref.shape[1]
    cols = pl.ds(pl.multiple_of(pl.program_id(0) * width, 128), width)
    out_ref[...] = dot(matrix_ref[...], normed_ref[:, cols]).astype(jnp.bfloat16)


def sum_of(first_ref, second_ref):
    total = first_ref[...].astype(jnp.float32) + second_ref[...].astype(jnp.float32)
    return total.astype(jnp.bfloat16)


def lean_pack_kernel(where, capacity, value_ref, gain_ref, ids_ref, out_ref, normed_ref, matrix_ref):
    @pl.when(pl.program_id(0) == 0)
    def _():
        normed_ref[...] = normalise(value_ref[...], gain_ref[...])
        matrix_ref[...] = slot_matrix(ids_ref[where], capacity, 0, capacity).astype(jnp.bfloat16)

    spread(matrix_ref, normed_ref, out_ref)


def sum_pack_kernel(
    first_ref,
    second_ref,
    gain_ref,
    matrix_ref,
    after_ref,
    own_turned_ref,
    other_turned_ref,
    value_ref,
    out_ref,
    normed_ref,
):
    @pl.when(pl.program_id(0) == 0)
    def _():
        value_ref[...] = sum_of(first_ref, second_ref)
        normed_ref[...] = normalise(value_ref[...], gain_ref[...])

    spread(matrix_ref, normed_ref, out_ref)


def wide_pack_kernel(
    where,
    capacity,
    own_ref,
    other_ref,
    gain_ref,
    ids_ref,
    other_ids_ref,
    after_ref,
    out_ref,
    normed_ref,
    matrix_ref,
):
    @pl.when(pl.program_id(0) == 0)
    def _():
        tokens = own_ref.shape[0]
        normed_ref[:tokens] = normalise(own_ref[...], gain_ref[...])
        normed_ref[tokens:] = normalise(other_ref[...], gain_ref[...])
        matrix_ref[...] = wide_matrix(ids_ref[where], other_ids_ref[where], capacity)

    spread(matrix_ref, normed_ref, out_ref)


def either_pack_kernel(
    flag_ref,
    own_ref,
    other_ref,
    own_first_ref,
    own_second_ref,
    other_first_ref,
    other_second_ref,
    gain_ref,
    matrix_ref,
    value_ref,
    out_ref,
    normed_ref,
):
    first = pl.program_id(0) == 0
    tokens = own_ref.shape[0]

    @pl.when(first & (flag_ref[0] == 0))
    def _():
        value_ref[...] = own_ref[...]
        normed_ref[:tokens] = normalise(own_ref[...], gain_ref[...])
        normed_ref[tokens:] = normalise(other_ref[...], gain_ref[...])

    @pl.when(first & (flag_ref[0] != 0))
    def _():
        value_ref[...] = sum_of(own_first_ref, own_second_ref)
        normed_ref[:tokens] = normalise(value_ref[...], gain_ref[...])
        normed_ref[tokens:] = normalise(sum_of(other_first_ref, other_second_ref), gain_ref[...])

    spread(matrix_ref, normed_ref, out_ref)


def expert_kernel(
    leg,
    deep,
    wide,
    rows_ref,
    gate_ref,
    up_ref,
    down_ref,
    after_ref,
    out_ref,
    rows,
    gate_cols,
    up_cols,
    down_rows,
    results,
    gate_sum,
    up_sum,
    active,
    rows_in,
    gate_in,
    up_in,
    down_in,
    results_out,
):
    arriving = []
    for number, cols in enumerate(deep):
        arriving.append(
            (
                pltpu.make_async_copy(rows_ref.at[:, cols], rows.at[:, cols], rows_in.at[number]),
                pltpu.make_async_copy(
                    gate_ref.at[leg, 0, cols], gate_cols.at[cols], gate_in.at[number]
                ),
                pltpu.make_async_copy(up_ref.at[leg, 0, cols], up_cols.at[cols], up_in.at[number]),
            )
        )
    for number, cols in enumerate(wide):
        arriving.append(
            (
                pltpu.make_async_copy(
                    down_ref.at[leg, 0, :, cols], down_rows.at[:, cols], down_in.at[number]
                ),
            )
        )
    for copies in arriving:
        for copy in copies:
            copy.start()
    for number, cols in enumerate(deep):
        for copy in arriving[number]:
            copy.wait()
        gate = dot(rows[:, cols], gate_cols[cols])
        up = dot(rows[:, cols], up_cols[cols])
        if number > 0:
            gate = gate + gate_sum[...]
            up = up + up_sum[...]
        if number < len(deep) - 1:
            gate_sum[...] = gate
            up_sum[...] = up
        else:
            active[...] = (jax.nn.silu(gate) * up).astype(jnp.bfloat16)
    leaving = []
    for number, cols in enumerate(wide):
        for copy in arriving[len(deep) + number]:
            copy.wait()
        results[:, cols] = dot(active[...], down_rows[:, cols]).astype(jnp.bfloat16)
        copy = pltpu.make_async_copy(
            results.at[:, cols], out_ref.at[:, cols], results_out.at[number]
        )
        copy.start()
        leaving.append(copy)
    for copy in leaving:
        copy.wait()


def combine_kernel(value_ref, rows_ref, matrix_ref, out_ref):
    tokens = out_ref.shape[0]
    terms = dot(matrix_ref[...], rows_ref[...])
    mixture = terms[:tokens] + terms[tokens:]
    out_ref[...] = (value_ref[...].astype(jnp.float32) + mixture).astype(jnp.bfloat16)


def last_combine_kernel(
    flag_ref, value_ref, rows_ref, matrix_ref, instead_ref, held_ref, out_ref
):
    combine_kernel(value_ref, rows_ref, matrix_ref, out_ref)

    @pl.when(flag_ref[0] != 0)
    def _():
        out_ref[...] = instead_ref[...]


def pair_combine_kernel(value_ref, rows_ref, matrix_ref, after_ref, own_ref, other_ref):
    tokens = own_ref.shape[0]
    terms = dot(matrix_ref[...], rows_ref[...])
    own = value_ref[...].astype(jnp.float32) + terms[:tokens] + terms[tokens : 2 * tokens]
    own_ref[...] = own.astype(own_ref.dtype)
    other = terms[2 * tokens : 3 * tokens] + terms[3 * tokens :]
    other_ref[...] = other.astype(jnp.bfloat16)


def halves_kernel(rows_ref, early_ref, late_ref):
    middle = early_ref.shape[0]
    early_ref[...] = rows_ref[:middle]
    late_ref[...] = rows_ref[middle:]


def add_kernel(own_ref, early_ref, late_ref, after_ref, out_ref):
    for number, back_ref in enumerate((early_ref, late_ref)):

        @pl.when(pl.program_id(0) == number)
        def _():
            out_ref[...] = sum_of(own_ref, back_ref)


def last_pair_kernel(own_ref, back_ref, out_ref):
    total = own_ref[...].astype(jnp.float32) + back_ref[...].astype(jnp.float32)
    out_ref[...] = total.astype(jnp.bfloat16)


def block_of(value, width):
    whole, index = value
    rows = whole.shape[-2]
    lead = len(index)
    return pl.BlockSpec((None,) * lead + (rows, width), lambda step: index + (0, step))


def all_of(value):
    whole, index = value
    lead = len(index)
    return pl.BlockSpec((None,) * lead + whole.shape[-2:], lambda step: index + (0, 0))


def plan(capacity, ids, weights, other_ids, other_weights, after):
    tokens = ids.shape[-1]
    lean, wide = EXPERTS * capacity, EXPERTS * 2 * capacity
    shapes = (
        (4 * tokens, wide),
        (2 * tokens, lean),
        (lean, tokens),
        (wide, 2 * tokens),
        (4 * tokens, wide),
        (2 * tokens, lean),
    )
    return pl.pallas_call(
        functools.partial(plan_kernel, capacity),
        grid=(1,),
        out_shape=[array(*shape) for shape in shapes],
        in_specs=[VMEM] * 4 + [ANY],
        out_specs=[pl.BlockSpec(shape, lambda step: (0, 0)) for shape in shapes],
        compiler_params=params(),
    )(ids, weights, other_ids, other_weights, after)


def pack(kernel, values, room, gain, others, scratch=(), flag=None, summed=False, work=0):
    rows, width = values[0][0].shape[-2:]
    block = split(width, 2)
    packed = pl.BlockSpec((room, block), lambda step: (0, step))
    whole = pl.BlockSpec((rows, width), lambda step: (0, 0))
    picks = flag is not None
    return pl.pallas_call(
        kernel,
        grid=(width // block,),
        out_shape=(array(rows, width), array(room, width)) if summed else array(room, width),
        in_specs=[SMEM] * picks
        + [all_of(value) for value in values]
        + [all_of(gain)]
        + [spec for _, spec in others],
        out_specs=(whole, packed) if summed else packed,
        scratch_shapes=scratch,
        compiler_params=params(),
        cost_estimate=pl.CostEstimate(flops=work, bytes_accessed=0, transcendentals=0)
        if work
        else None,
    )(*[flag] * picks, *[value[0] for value in values], gain[0], *[other for other, _ in others])


def combine(value, rows, matrix, last=None):
    width = rows.shape[1]
    tokens = matrix.shape[0] // 2
    block = split(width, 2)
    specs = [block_of(value, block), block_of((rows, ()), block), VMEM]
    args = [value[0], rows, matrix]
    if last is None:
        return pl.pallas_call(
            combine_kernel,
            grid=(width // block,),
            out_shape=array(tokens, width),
            in_specs=specs,
            out_specs=pl.BlockSpec((tokens, block), lambda step: (0, step)),
            compiler_params=params(),
        )(*args)
    flag, instead, held, leg = last
    return pl.pallas_call(
        last_combine_kernel,
        grid=(width // block,),
        out_shape=array(*held.shape),
        in_specs=[SMEM] + specs + [block_of((instead, ()), block), ANY],
        out_specs=pl.BlockSpec((None, None, tokens, block), lambda step: (leg, 0, 0, step)),
        input_output_aliases={5: 0},
        compiler_params=params(),
    )(flag, *args, instead, held)


def pair_combine(value, rows, matrix, after, kind):
    width = rows.shape[1]
    tokens = matrix.shape[0] // 4
    block = split(width, 2)
    part = pl.BlockSpec((tokens, block), lambda step: (0, step))
    return pl.pallas_call(
        pair_combine_kernel,
        grid=(width // block,),
        out_shape=(array(tokens, width, dtype=kind), array(tokens, width)),
        in_specs=[block_of(value, block), block_of((rows, ()), block), VMEM, ANY],
        out_specs=(part, part),
        compiler_params=params(),
    )(value[0], rows, matrix, after)


def last_pair(own, back, leg):
    tokens, width = own.shape
    block = split(width, 2)
    part = pl.BlockSpec((tokens, block), lambda step: (0, step))
    return pl.pallas_call(
        last_pair_kernel,
        grid=(width // block,),
        out_shape=array(2, 1, tokens, width),
        in_specs=[part, part],
        out_specs=pl.BlockSpec((None, None, tokens, block), lambda step: (leg, 0, 0, step)),
        compiler_params=params(),
    )(own, back)


def halves(rows):
    count, width = rows.shape
    block = split(width, 2)
    half = pl.BlockSpec((count // 2, block), lambda step: (0, step))
    return pl.pallas_call(
        halves_kernel,
        grid=(width // block,),
        out_shape=(array(count // 2, width),) * 2,
        in_specs=[pl.BlockSpec((count, block), lambda step: (0, step))],
        out_specs=(half, half),
        compiler_params=params(),
    )(rows)


def add(own, early, late, after):
    rows, width = early.shape
    half = pl.BlockSpec((rows, width), lambda step: (step, 0))
    whole = pl.BlockSpec((rows, width), lambda step: (0, 0))
    return pl.pallas_call(
        add_kernel,
        grid=(2,),
        out_shape=array(*own.shape),
        in_specs=[half, whole, whole, ANY],
        out_specs=half,
        compiler_params=params(),
    )(own, early, late, after)


def pieces(width, sizes):
    unit = width // 7
    if width % 7 or unit % 128:
        return [slice(0, width)]
    sizes = [size * unit for size in sizes]
    starts = [sum(sizes[:number]) for number in range(len(sizes))]
    return [slice(start, start + size) for start, size in zip(starts, sizes)]


def expert_pass(rows, leg, gate_cols, up_cols, down_rows, after, work):
    count, width = rows.shape
    hidden = gate_cols.shape[-1]
    deep = pieces(width, (1, 2, 2, 2) if count > 512 else (1,) * 7)
    wide = pieces(width, (2, 2, 2, 1))
    arrivals = pltpu.SemaphoreType.DMA((len(deep),))
    return pl.pallas_call(
        functools.partial(expert_kernel, leg, deep, wide),
        out_shape=array(count, width),
        in_specs=[ANY] * 5,
        out_specs=ANY,
        scratch_shapes=(
            pltpu.VMEM((count, width), jnp.bfloat16),
            pltpu.VMEM((width, hidden), jnp.bfloat16),
            pltpu.VMEM((width, hidden), jnp.bfloat16),
            pltpu.VMEM((hidden, width), jnp.bfloat16),
            pltpu.VMEM((count, width), jnp.bfloat16),
            pltpu.VMEM((count, hidden), jnp.float32),
            pltpu.VMEM((count, hidden), jnp.float32),
            pltpu.VMEM((count, hidden), jnp.bfloat16),
            arrivals,
            arrivals,
            arrivals,
            arrivals,
            arrivals,
        ),
        compiler_params=params(),
        cost_estimate=pl.CostEstimate(flops=work, bytes_accessed=0, transcendentals=0),
    )(rows, gate_cols, up_cols, down_rows, after)


def on_device(in_flight, routes, gate_weights, norm_gain, w_gate, w_up, w_down):
    section_count = lax.axis_size("pp")
    section_pos = lax.axis_index("pp")
    tokens, top_count = routes.shape[-2:]
    width = in_flight.shape[-1]
    capacity = tokens * top_count * 5 // (4 * EXPERTS)
    down = (in_flight, (0, 0))
    up = (in_flight, (1, 0))
    down_other = other_half(in_flight[0, 0])
    ids = jnp.swapaxes(routes[:, :, 0], -1, -2)
    weights = jnp.swapaxes(gate_weights[:, :, 0], -1, -2)
    other_ids = other_half(ids)
    other_weights = other_half(weights)
    gains = norm_gain[:, :, None]

    def experts(rows, leg, after, work):
        return expert_pass(rows, leg, w_gate, w_up, w_down, after, work)

    def worked(wide, wide_packed, lean, lean_own):
        wide_rows = within_column(wide_packed)
        early, late = halves(lean_own)
        early, late = other_half(early), other_half(late)
        part_own = experts(lean_own, lean, ids, 1)
        part_early = experts(early, lean, part_own, 1)
        wide_out = experts(wide_rows, wide, part_early, 1)
        part_late = experts(late, lean, wide_out, WORK)
        return within_column(wide_out), part_own, other_half(part_early), other_half(part_late)

    lean_rows, wide_rows = EXPERTS * capacity, EXPERTS * 2 * capacity
    packed = pack(
        functools.partial(lean_pack_kernel, (0, 1), capacity),
        [up],
        lean_rows,
        (gains, (1, 0)),
        [(ids, VMEM)],
        (pltpu.VMEM((tokens, width), jnp.bfloat16), pltpu.VMEM((lean_rows, tokens), jnp.bfloat16)),
    )
    lean_own = within_column(packed)
    packed = pack(
        functools.partial(wide_pack_kernel, (0, 0), capacity),
        [down, (down_other, ())],
        wide_rows,
        (gains, (0, 0)),
        [(ids, VMEM), (other_ids, VMEM), (other_weights, ANY)],
        (
            pltpu.VMEM((2 * tokens, width), jnp.bfloat16),
            pltpu.VMEM((wide_rows, 2 * tokens), jnp.bfloat16),
        ),
    )
    wide_back, part_own, early, late = worked(0, packed, 1, lean_own)
    plans = plan(capacity, ids, weights, other_ids, other_weights, part_own)
    wide_first, lean_first, lean_matrix, wide_matrix_next, wide_second, lean_second = plans
    lean_out = add(part_own, early, late, wide_first)
    lean_back = within_column(lean_out)
    own, other = pair_combine(down, wide_back, wide_first, lean_out, jnp.bfloat16)
    own_down, other_down = moved(own, 1, 0), moved(other, 1, 1)
    own_turned, other_turned = moved(own, 0, 1), moved(other, 0, 1)
    first_up = combine(up, lean_back, lean_first)
    descending, packed = pack(
        sum_pack_kernel,
        [(own_down, ()), (other_down, ())],
        lean_rows,
        (gains, (0, 0)),
        [(lean_matrix, VMEM), (first_up, ANY), (own_turned, ANY), (other_turned, ANY)],
        (pltpu.VMEM((tokens, width), jnp.bfloat16),),
        summed=True,
    )
    lean_own = within_column(packed)
    folds = (section_pos == section_count - 1).astype(jnp.int32).reshape(1)
    turned, packed = pack(
        either_pack_kernel,
        [
            (value, ())
            for value in (
                moved(first_up, -1, 0),
                moved(first_up, -1, 1),
                own,
                other_turned,
                own_turned,
                other,
            )
        ],
        wide_rows,
        (gains, (1, 0)),
        [(wide_matrix_next, VMEM)],
        (pltpu.VMEM((2 * tokens, width), jnp.bfloat16),),
        flag=folds,
        summed=True,
        work=WORK,
    )
    wide_back, part_own, early, late = worked(1, packed, 0, lean_own)
    lean_out = add(part_own, early, late, wide_second)
    lean_back = within_column(lean_out)
    own, other = pair_combine((turned, ()), wide_back, wide_second, lean_out, jnp.float32)
    result = last_pair(own, other_half(other), 1)
    starts = (section_pos == 0).astype(jnp.int32).reshape(1)
    return combine((descending, ()), lean_back, lean_second, (starts, first_up, result, 0))


def solution(mesh):
    placed = (
        P(None, "pp", "ep", None),
        P(None, None, "pp", "ep", None),
        P(None, None, "pp", "ep", None),
        P(None, "pp", None),
        P(None, "pp", None, "ep"),
        P(None, "pp", None, "ep"),
        P(None, "pp", "ep", None),
    )
    return jax.shard_map(
        on_device, mesh=mesh, in_specs=placed, out_specs=P(None, "pp", "ep", None), check_vma=False
    )
```

```python
import functools

import jax
import jax.numpy as jnp
from jax import lax
from jax.experimental import pallas as pl
from jax.experimental.pallas import tpu as pltpu
from jax.sharding import PartitionSpec as P

SIDE = 4
COLUMNS = (
    [SIDE * z + x for z in range(SIDE) for x in (0, 3)],
    [SIDE * z + x for z in range(SIDE) for x in (1, 2)],
)
EXPERTS = 2 * SIDE
ROOM = 127 * 2**19
WORK = 5 * 10**10
VMEM = pl.BlockSpec(memory_space=pltpu.VMEM)
SMEM = pl.BlockSpec(memory_space=pltpu.SMEM)
ANY = pl.BlockSpec(memory_space=pl.ANY)


def moved(value, steps, crossed):
    sections, places = lax.axis_size("pp"), lax.axis_size("ep")
    if steps == 0:
        sources = [sections - 1]
    else:
        sources = [section for section in range(sections) if 0 <= section + steps < sections]
    pairs = [
        (section * places + place, (section + steps) * places + (place ^ crossed))
        for section in sources
        for place in range(places)
    ]
    return lax.ppermute(value, ("pp", "ep"), pairs)


def other_half(value):
    return lax.ppermute(value, "ep", [(place, place ^ 1) for place in range(lax.axis_size("ep"))])


def within_column(rows):
    shape = rows.shape
    received = lax.all_to_all(
        rows.reshape(EXPERTS, shape[0] // EXPERTS, shape[1]),
        "ep",
        split_axis=0,
        concat_axis=0,
        tiled=True,
        axis_index_groups=COLUMNS,
    )
    return received.reshape(shape)


def iota(shape, dim):
    return lax.broadcasted_iota(jnp.int32, shape, dim)


def dot(left, right):
    return jnp.dot(left, right, preferred_element_type=jnp.float32)


def array(*shape, dtype=jnp.bfloat16):
    return jax.ShapeDtypeStruct(shape, dtype)


def split(width, parts):
    return width // parts if width % (128 * parts) == 0 else width


def params():
    return pltpu.CompilerParams(vmem_limit_bytes=ROOM)


def normalise(value, gain):
    widened = value.astype(jnp.float32)
    scale = lax.rsqrt(jnp.mean(widened * widened, axis=-1, keepdims=True) + 1e-06)
    return (widened * scale * gain).astype(jnp.bfloat16)


def slots(ids):
    tokens = ids.shape[1]
    expert = iota((EXPERTS, tokens), 0)
    named = (ids[0:1] == expert) | (ids[1:2] == expert)
    before = (iota((tokens, tokens), 0) < iota((tokens, tokens), 1)).astype(jnp.bfloat16)
    earlier = dot(jnp.where(named, 1.0, 0.0).astype(jnp.bfloat16), before)
    return jnp.where(named, earlier, -1.0)


def slot_matrix(ids, capacity, first, room, weights=None):
    tokens = ids.shape[1]
    slot = slots(ids)
    place = iota((EXPERTS, room, tokens), 1).astype(jnp.float32) - float(first)
    if weights is None:
        value = 1.0
    else:
        expert = iota((EXPERTS, tokens), 0)
        value = jnp.where(ids[0:1] == expert, weights[0:1], 0.0) + jnp.where(
            ids[1:2] == expert, weights[1:2], 0.0
        )
        value = value[:, None, :]
    chosen = (slot[:, None, :] == place) & (place >= 0.0)
    return jnp.where(chosen, value, 0.0).reshape(EXPERTS * room, tokens)


def two_terms(matrix):
    high = matrix.astype(jnp.bfloat16)
    return high, (matrix - high.astype(jnp.float32)).astype(jnp.bfloat16)


def across(matrix):
    rows, tokens = matrix.shape
    extra = -rows % 128
    if extra:
        matrix = jnp.concatenate([matrix, jnp.zeros((extra, tokens), matrix.dtype)], axis=0)
    return matrix.T[:, :rows]


def wide_matrix(ids, other_ids, capacity):
    room = 2 * capacity
    own = slot_matrix(ids, capacity, 0, room)
    other = slot_matrix(other_ids, capacity, capacity, room)
    return jnp.concatenate([own, other], axis=1).astype(jnp.bfloat16)


def lean_weight_matrix(ids, weights, capacity):
    return jnp.concatenate(
        two_terms(across(slot_matrix(ids, capacity, 0, capacity, weights))), axis=0
    )


def wide_weight_matrix(ids, weights, other_ids, other_weights, capacity):
    room = 2 * capacity
    own = two_terms(across(slot_matrix(ids, capacity, 0, room, weights)))
    other = two_terms(across(slot_matrix(other_ids, capacity, capacity, room, other_weights)))
    return jnp.concatenate(own + other, axis=0)


def plan_kernel(
    capacity,
    ids_ref,
    weights_ref,
    other_ids_ref,
    other_weights_ref,
    after_ref,
    wide_first,
    lean_first,
    lean_rows,
    wide_rows,
    wide_second,
    lean_second,
):
    def wide(tick):
        place = (tick, tick)
        return wide_weight_matrix(
            ids_ref[place],
            weights_ref[place],
            other_ids_ref[place],
            other_weights_ref[place],
            capacity,
        )

    def lean(tick):
        place = (tick, 1 - tick)
        return lean_weight_matrix(ids_ref[place], weights_ref[place], capacity)

    wide_first[...], lean_first[...] = wide(0), lean(0)
    wide_second[...], lean_second[...] = wide(1), lean(1)
    lean_rows[...] = slot_matrix(ids_ref[1, 0], capacity, 0, capacity).astype(jnp.bfloat16)
    wide_rows[...] = wide_matrix(ids_ref[1, 1], other_ids_ref[1, 1], capacity)


def spread(matrix_ref, normed_ref, out_ref):
    width = out_ref.shape[1]
    cols = pl.ds(pl.multiple_of(pl.program_id(0) * width, 128), width)
    out_ref[...] = dot(matrix_ref[...], normed_ref[:, cols]).astype(jnp.bfloat16)


def sum_of(first_ref, second_ref):
    total = first_ref[...].astype(jnp.float32) + second_ref[...].astype(jnp.float32)
    return total.astype(jnp.bfloat16)


def lean_pack_kernel(where, capacity, value_ref, gain_ref, ids_ref, out_ref, normed_ref, matrix_ref):
    @pl.when(pl.program_id(0) == 0)
    def _():
        normed_ref[...] = normalise(value_ref[...], gain_ref[...])
        matrix_ref[...] = slot_matrix(ids_ref[where], capacity, 0, capacity).astype(jnp.bfloat16)

    spread(matrix_ref, normed_ref, out_ref)


def sum_pack_kernel(
    first_ref,
    second_ref,
    gain_ref,
    matrix_ref,
    after_ref,
    own_turned_ref,
    other_turned_ref,
    value_ref,
    out_ref,
    normed_ref,
):
    @pl.when(pl.program_id(0) == 0)
    def _():
        value_ref[...] = sum_of(first_ref, second_ref)
        normed_ref[...] = normalise(value_ref[...], gain_ref[...])

    spread(matrix_ref, normed_ref, out_ref)


def wide_pack_kernel(
    where,
    capacity,
    own_ref,
    other_ref,
    gain_ref,
    ids_ref,
    other_ids_ref,
    after_ref,
    out_ref,
    normed_ref,
    matrix_ref,
):
    @pl.when(pl.program_id(0) == 0)
    def _():
        tokens = own_ref.shape[0]
        normed_ref[:tokens] = normalise(own_ref[...], gain_ref[...])
        normed_ref[tokens:] = normalise(other_ref[...], gain_ref[...])
        matrix_ref[...] = wide_matrix(ids_ref[where], other_ids_ref[where], capacity)

    spread(matrix_ref, normed_ref, out_ref)


def either_pack_kernel(
    flag_ref,
    own_ref,
    other_ref,
    own_first_ref,
    own_second_ref,
    other_first_ref,
    other_second_ref,
    gain_ref,
    matrix_ref,
    value_ref,
    out_ref,
    normed_ref,
):
    first = pl.program_id(0) == 0
    tokens = own_ref.shape[0]

    @pl.when(first & (flag_ref[0] == 0))
    def _():
        value_ref[...] = own_ref[...]
        normed_ref[:tokens] = normalise(own_ref[...], gain_ref[...])
        normed_ref[tokens:] = normalise(other_ref[...], gain_ref[...])

    @pl.when(first & (flag_ref[0] != 0))
    def _():
        value_ref[...] = sum_of(own_first_ref, own_second_ref)
        normed_ref[:tokens] = normalise(value_ref[...], gain_ref[...])
        normed_ref[tokens:] = normalise(sum_of(other_first_ref, other_second_ref), gain_ref[...])

    spread(matrix_ref, normed_ref, out_ref)


def expert_kernel(
    leg,
    deep,
    wide,
    rows_ref,
    gate_ref,
    up_ref,
    down_ref,
    after_ref,
    out_ref,
    rows,
    gate_cols,
    up_cols,
    down_rows,
    results,
    gate_sum,
    up_sum,
    active,
    rows_in,
    gate_in,
    up_in,
    down_in,
    results_out,
):
    arriving = []
    for number, cols in enumerate(deep):
        arriving.append(
            (
                pltpu.make_async_copy(rows_ref.at[:, cols], rows.at[:, cols], rows_in.at[number]),
                pltpu.make_async_copy(
                    gate_ref.at[leg, 0, cols], gate_cols.at[cols], gate_in.at[number]
                ),
                pltpu.make_async_copy(up_ref.at[leg, 0, cols], up_cols.at[cols], up_in.at[number]),
            )
        )
    for number, cols in enumerate(wide):
        arriving.append(
            (
                pltpu.make_async_copy(
                    down_ref.at[leg, 0, :, cols], down_rows.at[:, cols], down_in.at[number]
                ),
            )
        )
    for copies in arriving:
        for copy in copies:
            copy.start()
    for number, cols in enumerate(deep):
        for copy in arriving[number]:
            copy.wait()
        gate = dot(rows[:, cols], gate_cols[cols])
        up = dot(rows[:, cols], up_cols[cols])
        if number > 0:
            gate = gate + gate_sum[...]
            up = up + up_sum[...]
        if number < len(deep) - 1:
            gate_sum[...] = gate
            up_sum[...] = up
        else:
            active[...] = (jax.nn.silu(gate) * up).astype(jnp.bfloat16)
    leaving = []
    for number, cols in enumerate(wide):
        for copy in arriving[len(deep) + number]:
            copy.wait()
        results[:, cols] = dot(active[...], down_rows[:, cols]).astype(jnp.bfloat16)
        copy = pltpu.make_async_copy(
            results.at[:, cols], out_ref.at[:, cols], results_out.at[number]
        )
        copy.start()
        leaving.append(copy)
    for copy in leaving:
        copy.wait()


def combine_kernel(value_ref, rows_ref, matrix_ref, out_ref):
    tokens = out_ref.shape[0]
    terms = dot(matrix_ref[...], rows_ref[...])
    mixture = terms[:tokens] + terms[tokens:]
    out_ref[...] = (value_ref[...].astype(jnp.float32) + mixture).astype(jnp.bfloat16)


def last_kernel(
    flag_ref, value_ref, rows_ref, matrix_ref, instead_ref, own_ref, back_ref, out_ref
):
    combine_kernel(value_ref, rows_ref, matrix_ref, out_ref.at[0])
    out_ref[1] = sum_of(own_ref, back_ref)

    @pl.when(flag_ref[0] != 0)
    def _():
        out_ref[0] = instead_ref[...]


def pair_combine_kernel(value_ref, rows_ref, matrix_ref, after_ref, own_ref, other_ref):
    tokens = own_ref.shape[0]
    terms = dot(matrix_ref[...], rows_ref[...])
    own = value_ref[...].astype(jnp.float32) + terms[:tokens] + terms[tokens : 2 * tokens]
    own_ref[...] = own.astype(own_ref.dtype)
    other = terms[2 * tokens : 3 * tokens] + terms[3 * tokens :]
    other_ref[...] = other.astype(jnp.bfloat16)


def other_kernel(rows_ref, matrix_ref, after_ref, out_ref):
    tokens = out_ref.shape[0]
    terms = dot(matrix_ref[...], rows_ref[...])
    out_ref[...] = (terms[:tokens] + terms[tokens:]).astype(jnp.bfloat16)


def own_kernel(value_ref, rows_ref, matrix_ref, after_ref, out_ref):
    tokens = out_ref.shape[0]
    terms = dot(matrix_ref[...], rows_ref[...])
    total = value_ref[...].astype(jnp.float32) + terms[:tokens] + terms[tokens:]
    out_ref[...] = total.astype(out_ref.dtype)


def halves_kernel(rows_ref, early_ref, late_ref):
    middle = early_ref.shape[0]
    early_ref[...] = rows_ref[:middle]
    late_ref[...] = rows_ref[middle:]


def add_kernel(own_ref, early_ref, late_ref, after_ref, out_ref):
    for number, back_ref in enumerate((early_ref, late_ref)):

        @pl.when(pl.program_id(0) == number)
        def _():
            out_ref[...] = sum_of(own_ref, back_ref)


def block_of(value, width):
    whole, index = value
    rows = whole.shape[-2]
    lead = len(index)
    return pl.BlockSpec((None,) * lead + (rows, width), lambda step: index + (0, step))


def all_of(value):
    whole, index = value
    lead = len(index)
    return pl.BlockSpec((None,) * lead + whole.shape[-2:], lambda step: index + (0, 0))


def plan(capacity, ids, weights, other_ids, other_weights, after):
    tokens = ids.shape[-1]
    lean, wide = EXPERTS * capacity, EXPERTS * 2 * capacity
    shapes = (
        (4 * tokens, wide),
        (2 * tokens, lean),
        (lean, tokens),
        (wide, 2 * tokens),
        (4 * tokens, wide),
        (2 * tokens, lean),
    )
    return pl.pallas_call(
        functools.partial(plan_kernel, capacity),
        grid=(1,),
        out_shape=[array(*shape) for shape in shapes],
        in_specs=[VMEM] * 4 + [ANY],
        out_specs=[pl.BlockSpec(shape, lambda step: (0, 0)) for shape in shapes],
        compiler_params=params(),
    )(ids, weights, other_ids, other_weights, after)


def pack(kernel, values, room, gain, others, scratch=(), flag=None, summed=False, work=0):
    rows, width = values[0][0].shape[-2:]
    block = split(width, 2)
    packed = pl.BlockSpec((room, block), lambda step: (0, step))
    whole = pl.BlockSpec((rows, width), lambda step: (0, 0))
    picks = flag is not None
    return pl.pallas_call(
        kernel,
        grid=(width // block,),
        out_shape=(array(rows, width), array(room, width)) if summed else array(room, width),
        in_specs=[SMEM] * picks
        + [all_of(value) for value in values]
        + [all_of(gain)]
        + [spec for _, spec in others],
        out_specs=(whole, packed) if summed else packed,
        scratch_shapes=scratch,
        compiler_params=params(),
        cost_estimate=pl.CostEstimate(flops=work, bytes_accessed=0, transcendentals=0)
        if work
        else None,
    )(*[flag] * picks, *[value[0] for value in values], gain[0], *[other for other, _ in others])


def combine(value, rows, matrix):
    width = rows.shape[1]
    tokens = matrix.shape[0] // 2
    block = split(width, 2)
    return pl.pallas_call(
        combine_kernel,
        grid=(width // block,),
        out_shape=array(tokens, width),
        in_specs=[block_of(value, block), block_of((rows, ()), block), VMEM],
        out_specs=pl.BlockSpec((tokens, block), lambda step: (0, step)),
        compiler_params=params(),
    )(value[0], rows, matrix)


def last(flag, value, rows, matrix, instead, own, back):
    width = rows.shape[1]
    tokens = matrix.shape[0] // 2
    block = split(width, 2)
    part = pl.BlockSpec((tokens, block), lambda step: (0, step))
    return pl.pallas_call(
        last_kernel,
        grid=(width // block,),
        out_shape=array(2, 1, tokens, width),
        in_specs=[SMEM, part, block_of((rows, ()), block), VMEM, part, part, part],
        out_specs=pl.BlockSpec((2, None, tokens, block), lambda step: (0, 0, 0, step)),
        compiler_params=params(),
    )(flag, value, rows, matrix, instead, own, back)


def pair_combine(value, rows, matrix, after, kind):
    width = rows.shape[1]
    tokens = matrix.shape[0] // 4
    block = split(width, 2)
    part = pl.BlockSpec((tokens, block), lambda step: (0, step))
    return pl.pallas_call(
        pair_combine_kernel,
        grid=(width // block,),
        out_shape=(array(tokens, width, dtype=kind), array(tokens, width)),
        in_specs=[block_of(value, block), block_of((rows, ()), block), VMEM, ANY],
        out_specs=(part, part),
        compiler_params=params(),
    )(value[0], rows, matrix, after)


def other_then_own(value, rows, matrix, after, kind):
    room, width = rows.shape
    tokens = matrix.shape[0] // 4
    block = split(width, 2)
    part = pl.BlockSpec((tokens, block), lambda step: (0, step))

    def weights_at(number):
        return pl.BlockSpec((2 * tokens, room), lambda step: (number, 0))

    other = pl.pallas_call(
        other_kernel,
        grid=(width // block,),
        out_shape=array(tokens, width),
        in_specs=[block_of((rows, ()), block), weights_at(1), ANY],
        out_specs=part,
        compiler_params=params(),
    )(rows, matrix, after)
    own = pl.pallas_call(
        own_kernel,
        grid=(width // block,),
        out_shape=array(tokens, width, dtype=kind),
        in_specs=[block_of(value, block), block_of((rows, ()), block), weights_at(0), ANY],
        out_specs=part,
        compiler_params=params(),
    )(value[0], rows, matrix, other)
    return own, other


def halves(rows):
    count, width = rows.shape
    block = split(width, 2)
    half = pl.BlockSpec((count // 2, block), lambda step: (0, step))
    return pl.pallas_call(
        halves_kernel,
        grid=(width // block,),
        out_shape=(array(count // 2, width),) * 2,
        in_specs=[pl.BlockSpec((count, block), lambda step: (0, step))],
        out_specs=(half, half),
        compiler_params=params(),
    )(rows)


def add(own, early, late, after):
    rows, width = early.shape
    half = pl.BlockSpec((rows, width), lambda step: (step, 0))
    whole = pl.BlockSpec((rows, width), lambda step: (0, 0))
    return pl.pallas_call(
        add_kernel,
        grid=(2,),
        out_shape=array(*own.shape),
        in_specs=[half, whole, whole, ANY],
        out_specs=half,
        compiler_params=params(),
    )(own, early, late, after)


def pieces(width, sizes):
    unit = width // 7
    if width % 7 or unit % 128:
        return [slice(0, width)]
    sizes = [size * unit for size in sizes]
    starts = [sum(sizes[:number]) for number in range(len(sizes))]
    return [slice(start, start + size) for start, size in zip(starts, sizes)]


def expert_pass(rows, leg, gate_cols, up_cols, down_rows, after, work):
    count, width = rows.shape
    hidden = gate_cols.shape[-1]
    deep = pieces(width, (1, 2, 2, 2) if count > 512 else (1,) * 7)
    wide = pieces(width, (2, 2, 2, 1))
    arrivals = pltpu.SemaphoreType.DMA((len(deep),))
    return pl.pallas_call(
        functools.partial(expert_kernel, leg, deep, wide),
        out_shape=array(count, width),
        in_specs=[ANY] * 5,
        out_specs=ANY,
        scratch_shapes=(
            pltpu.VMEM((count, width), jnp.bfloat16),
            pltpu.VMEM((width, hidden), jnp.bfloat16),
            pltpu.VMEM((width, hidden), jnp.bfloat16),
            pltpu.VMEM((hidden, width), jnp.bfloat16),
            pltpu.VMEM((count, width), jnp.bfloat16),
            pltpu.VMEM((count, hidden), jnp.float32),
            pltpu.VMEM((count, hidden), jnp.float32),
            pltpu.VMEM((count, hidden), jnp.bfloat16),
            arrivals,
            arrivals,
            arrivals,
            arrivals,
            arrivals,
        ),
        compiler_params=params(),
        cost_estimate=pl.CostEstimate(flops=work, bytes_accessed=0, transcendentals=0),
    )(rows, gate_cols, up_cols, down_rows, after)


def on_device(in_flight, routes, gate_weights, norm_gain, w_gate, w_up, w_down):
    section_count = lax.axis_size("pp")
    section_pos = lax.axis_index("pp")
    tokens, top_count = routes.shape[-2:]
    width = in_flight.shape[-1]
    capacity = tokens * top_count * 5 // (4 * EXPERTS)
    down = (in_flight, (0, 0))
    up = (in_flight, (1, 0))
    down_other = other_half(in_flight[0, 0])
    ids = jnp.swapaxes(routes[:, :, 0], -1, -2)
    weights = jnp.swapaxes(gate_weights[:, :, 0], -1, -2)
    other_ids = other_half(ids)
    other_weights = other_half(weights)
    gains = norm_gain[:, :, None]

    def experts(rows, leg, after, work):
        return expert_pass(rows, leg, w_gate, w_up, w_down, after, work)

    def worked(wide, wide_packed, lean, lean_own):
        wide_rows = within_column(wide_packed)
        early, late = halves(lean_own)
        early, late = other_half(early), other_half(late)
        part_own = experts(lean_own, lean, ids, 1)
        part_early = experts(early, lean, part_own, 1)
        wide_out = experts(wide_rows, wide, part_early, 1)
        part_late = experts(late, lean, wide_out, WORK)
        return within_column(wide_out), part_own, other_half(part_early), other_half(part_late)

    lean_rows, wide_rows = EXPERTS * capacity, EXPERTS * 2 * capacity
    packed = pack(
        functools.partial(lean_pack_kernel, (0, 1), capacity),
        [up],
        lean_rows,
        (gains, (1, 0)),
        [(ids, VMEM)],
        (pltpu.VMEM((tokens, width), jnp.bfloat16), pltpu.VMEM((lean_rows, tokens), jnp.bfloat16)),
    )
    lean_own = within_column(packed)
    packed = pack(
        functools.partial(wide_pack_kernel, (0, 0), capacity),
        [down, (down_other, ())],
        wide_rows,
        (gains, (0, 0)),
        [(ids, VMEM), (other_ids, VMEM), (other_weights, ANY)],
        (
            pltpu.VMEM((2 * tokens, width), jnp.bfloat16),
            pltpu.VMEM((wide_rows, 2 * tokens), jnp.bfloat16),
        ),
    )
    wide_back, part_own, early, late = worked(0, packed, 1, lean_own)
    plans = plan(capacity, ids, weights, other_ids, other_weights, part_own)
    wide_first, lean_first, lean_matrix, wide_matrix_next, wide_second, lean_second = plans
    lean_out = add(part_own, early, late, wide_first)
    lean_back = within_column(lean_out)
    own, other = pair_combine(down, wide_back, wide_first, lean_out, jnp.bfloat16)
    own_down, other_down = moved(own, 1, 0), moved(other, 1, 1)
    own_turned, other_turned = moved(own, 0, 1), moved(other, 0, 1)
    first_up = combine(up, lean_back, lean_first)
    descending, packed = pack(
        sum_pack_kernel,
        [(own_down, ()), (other_down, ())],
        lean_rows,
        (gains, (0, 0)),
        [(lean_matrix, VMEM), (first_up, ANY), (own_turned, ANY), (other_turned, ANY)],
        (pltpu.VMEM((tokens, width), jnp.bfloat16),),
        summed=True,
    )
    lean_own = within_column(packed)
    folds = (section_pos == section_count - 1).astype(jnp.int32).reshape(1)
    turned, packed = pack(
        either_pack_kernel,
        [
            (value, ())
            for value in (
                moved(first_up, -1, 0),
                moved(first_up, -1, 1),
                own,
                other_turned,
                own_turned,
                other,
            )
        ],
        wide_rows,
        (gains, (1, 0)),
        [(wide_matrix_next, VMEM)],
        (pltpu.VMEM((2 * tokens, width), jnp.bfloat16),),
        flag=folds,
        summed=True,
        work=WORK,
    )
    wide_back, part_own, early, late = worked(1, packed, 0, lean_own)
    lean_out = add(part_own, early, late, wide_second)
    lean_back = within_column(lean_out)
    own, other = other_then_own((turned, ()), wide_back, wide_second, lean_out, jnp.float32)
    starts = (section_pos == 0).astype(jnp.int32).reshape(1)
    return last(starts, descending, lean_back, lean_second, first_up, own, other_half(other))


def solution(mesh):
    placed = (
        P(None, "pp", "ep", None),
        P(None, None, "pp", "ep", None),
        P(None, None, "pp", "ep", None),
        P(None, "pp", None),
        P(None, "pp", None, "ep"),
        P(None, "pp", None, "ep"),
        P(None, "pp", "ep", None),
    )
    return jax.shard_map(
        on_device, mesh=mesh, in_specs=placed, out_specs=P(None, "pp", "ep", None), check_vma=False
    )
```

```python
import functools

import jax
import jax.numpy as jnp
from jax import lax
from jax.experimental import pallas as pl
from jax.experimental.pallas import tpu as pltpu
from jax.sharding import PartitionSpec as P

SIDE = 4
COLUMNS = (
    [SIDE * z + x for z in range(SIDE) for x in (0, 3)],
    [SIDE * z + x for z in range(SIDE) for x in (1, 2)],
)
EXPERTS = 2 * SIDE
ROOM = 127 * 2**19
WORK = 5 * 10**10
VMEM = pl.BlockSpec(memory_space=pltpu.VMEM)
SMEM = pl.BlockSpec(memory_space=pltpu.SMEM)
ANY = pl.BlockSpec(memory_space=pl.ANY)


def moved(value, steps, crossed):
    sections, places = lax.axis_size("pp"), lax.axis_size("ep")
    if steps == 0:
        sources = [sections - 1]
    else:
        sources = [section for section in range(sections) if 0 <= section + steps < sections]
    pairs = [
        (section * places + place, (section + steps) * places + (place ^ crossed))
        for section in sources
        for place in range(places)
    ]
    return lax.ppermute(value, ("pp", "ep"), pairs)


def other_half(value):
    return lax.ppermute(value, "ep", [(place, place ^ 1) for place in range(lax.axis_size("ep"))])


def within_column(rows):
    shape = rows.shape
    received = lax.all_to_all(
        rows.reshape(EXPERTS, shape[0] // EXPERTS, shape[1]),
        "ep",
        split_axis=0,
        concat_axis=0,
        tiled=True,
        axis_index_groups=COLUMNS,
    )
    return received.reshape(shape)


def iota(shape, dim):
    return lax.broadcasted_iota(jnp.int32, shape, dim)


def dot(left, right):
    return jnp.dot(left, right, preferred_element_type=jnp.float32)


def array(*shape, dtype=jnp.bfloat16):
    return jax.ShapeDtypeStruct(shape, dtype)


def split(width, parts):
    return width // parts if width % (128 * parts) == 0 else width


def params():
    return pltpu.CompilerParams(vmem_limit_bytes=ROOM)


def normalise(value, gain):
    widened = value.astype(jnp.float32)
    scale = lax.rsqrt(jnp.mean(widened * widened, axis=-1, keepdims=True) + 1e-06)
    return (widened * scale * gain).astype(jnp.bfloat16)


def slots(ids):
    tokens = ids.shape[1]
    expert = iota((EXPERTS, tokens), 0)
    named = (ids[0:1] == expert) | (ids[1:2] == expert)
    before = (iota((tokens, tokens), 0) < iota((tokens, tokens), 1)).astype(jnp.bfloat16)
    earlier = dot(jnp.where(named, 1.0, 0.0).astype(jnp.bfloat16), before)
    return jnp.where(named, earlier, -1.0)


def slot_matrix(ids, capacity, first, room, weights=None):
    tokens = ids.shape[1]
    slot = slots(ids)
    place = iota((EXPERTS, room, tokens), 1).astype(jnp.float32) - float(first)
    if weights is None:
        value = 1.0
    else:
        expert = iota((EXPERTS, tokens), 0)
        value = jnp.where(ids[0:1] == expert, weights[0:1], 0.0) + jnp.where(
            ids[1:2] == expert, weights[1:2], 0.0
        )
        value = value[:, None, :]
    chosen = (slot[:, None, :] == place) & (place >= 0.0)
    return jnp.where(chosen, value, 0.0).reshape(EXPERTS * room, tokens)


def two_terms(matrix):
    high = matrix.astype(jnp.bfloat16)
    return high, (matrix - high.astype(jnp.float32)).astype(jnp.bfloat16)


def across(matrix):
    rows, tokens = matrix.shape
    extra = -rows % 128
    if extra:
        matrix = jnp.concatenate([matrix, jnp.zeros((extra, tokens), matrix.dtype)], axis=0)
    return matrix.T[:, :rows]


def wide_matrix(ids, other_ids, capacity):
    room = 2 * capacity
    own = slot_matrix(ids, capacity, 0, room)
    other = slot_matrix(other_ids, capacity, capacity, room)
    return jnp.concatenate([own, other], axis=1).astype(jnp.bfloat16)


def lean_weight_matrix(ids, weights, capacity):
    return jnp.concatenate(
        two_terms(across(slot_matrix(ids, capacity, 0, capacity, weights))), axis=0
    )


def wide_weight_matrix(ids, weights, other_ids, other_weights, capacity):
    room = 2 * capacity
    own = two_terms(across(slot_matrix(ids, capacity, 0, room, weights)))
    other = two_terms(across(slot_matrix(other_ids, capacity, capacity, room, other_weights)))
    return jnp.concatenate(own + other, axis=0)


def plan_kernel(
    capacity,
    ids_ref,
    weights_ref,
    other_ids_ref,
    other_weights_ref,
    after_ref,
    wide_first,
    lean_first,
    lean_rows,
    wide_rows,
    wide_second,
    lean_second,
):
    def wide(tick):
        place = (tick, tick)
        return wide_weight_matrix(
            ids_ref[place],
            weights_ref[place],
            other_ids_ref[place],
            other_weights_ref[place],
            capacity,
        )

    def lean(tick):
        place = (tick, 1 - tick)
        return lean_weight_matrix(ids_ref[place], weights_ref[place], capacity)

    wide_first[...], lean_first[...] = wide(0), lean(0)
    wide_second[...], lean_second[...] = wide(1), lean(1)
    lean_rows[...] = slot_matrix(ids_ref[1, 0], capacity, 0, capacity).astype(jnp.bfloat16)
    wide_rows[...] = wide_matrix(ids_ref[1, 1], other_ids_ref[1, 1], capacity)


def spread(matrix_ref, normed_ref, out_ref):
    width = out_ref.shape[1]
    cols = pl.ds(pl.multiple_of(pl.program_id(0) * width, 128), width)
    out_ref[...] = dot(matrix_ref[...], normed_ref[:, cols]).astype(jnp.bfloat16)


def sum_of(first_ref, second_ref):
    total = first_ref[...].astype(jnp.float32) + second_ref[...].astype(jnp.float32)
    return total.astype(jnp.bfloat16)


def lean_pack_kernel(where, capacity, value_ref, gain_ref, ids_ref, out_ref, normed_ref, matrix_ref):
    @pl.when(pl.program_id(0) == 0)
    def _():
        normed_ref[...] = normalise(value_ref[...], gain_ref[...])
        matrix_ref[...] = slot_matrix(ids_ref[where], capacity, 0, capacity).astype(jnp.bfloat16)

    spread(matrix_ref, normed_ref, out_ref)


def sum_pack_kernel(
    first_ref,
    second_ref,
    gain_ref,
    matrix_ref,
    after_ref,
    own_turned_ref,
    other_turned_ref,
    value_ref,
    out_ref,
    normed_ref,
):
    @pl.when(pl.program_id(0) == 0)
    def _():
        value_ref[...] = sum_of(first_ref, second_ref)
        normed_ref[...] = normalise(value_ref[...], gain_ref[...])

    spread(matrix_ref, normed_ref, out_ref)


def wide_pack_kernel(
    where,
    capacity,
    own_ref,
    other_ref,
    gain_ref,
    ids_ref,
    other_ids_ref,
    after_ref,
    out_ref,
    normed_ref,
    matrix_ref,
):
    @pl.when(pl.program_id(0) == 0)
    def _():
        tokens = own_ref.shape[0]
        normed_ref[:tokens] = normalise(own_ref[...], gain_ref[...])
        normed_ref[tokens:] = normalise(other_ref[...], gain_ref[...])
        matrix_ref[...] = wide_matrix(ids_ref[where], other_ids_ref[where], capacity)

    spread(matrix_ref, normed_ref, out_ref)


def either_pack_kernel(
    flag_ref,
    own_ref,
    other_ref,
    own_first_ref,
    own_second_ref,
    other_first_ref,
    other_second_ref,
    gain_ref,
    matrix_ref,
    value_ref,
    out_ref,
    normed_ref,
):
    first = pl.program_id(0) == 0
    tokens = own_ref.shape[0]

    @pl.when(first & (flag_ref[0] == 0))
    def _():
        value_ref[...] = own_ref[...]
        normed_ref[:tokens] = normalise(own_ref[...], gain_ref[...])
        normed_ref[tokens:] = normalise(other_ref[...], gain_ref[...])

    @pl.when(first & (flag_ref[0] != 0))
    def _():
        value_ref[...] = sum_of(own_first_ref, own_second_ref)
        normed_ref[:tokens] = normalise(value_ref[...], gain_ref[...])
        normed_ref[tokens:] = normalise(sum_of(other_first_ref, other_second_ref), gain_ref[...])

    spread(matrix_ref, normed_ref, out_ref)


def expert_kernel(
    leg,
    deep,
    wide,
    rows_ref,
    gate_ref,
    up_ref,
    down_ref,
    after_ref,
    out_ref,
    rows,
    gate_cols,
    up_cols,
    down_rows,
    results,
    gate_sum,
    up_sum,
    active,
    rows_in,
    gate_in,
    up_in,
    down_in,
    results_out,
):
    arriving = []
    for number, cols in enumerate(deep):
        arriving.append(
            (
                pltpu.make_async_copy(rows_ref.at[:, cols], rows.at[:, cols], rows_in.at[number]),
                pltpu.make_async_copy(
                    gate_ref.at[leg, 0, cols], gate_cols.at[cols], gate_in.at[number]
                ),
                pltpu.make_async_copy(up_ref.at[leg, 0, cols], up_cols.at[cols], up_in.at[number]),
            )
        )
    for number, cols in enumerate(wide):
        arriving.append(
            (
                pltpu.make_async_copy(
                    down_ref.at[leg, 0, :, cols], down_rows.at[:, cols], down_in.at[number]
                ),
            )
        )
    for copies in arriving:
        for copy in copies:
            copy.start()
    for number, cols in enumerate(deep):
        for copy in arriving[number]:
            copy.wait()
        gate = dot(rows[:, cols], gate_cols[cols])
        up = dot(rows[:, cols], up_cols[cols])
        if number > 0:
            gate = gate + gate_sum[...]
            up = up + up_sum[...]
        if number < len(deep) - 1:
            gate_sum[...] = gate
            up_sum[...] = up
        else:
            active[...] = (jax.nn.silu(gate) * up).astype(jnp.bfloat16)
    leaving = []
    for number, cols in enumerate(wide):
        for copy in arriving[len(deep) + number]:
            copy.wait()
        results[:, cols] = dot(active[...], down_rows[:, cols]).astype(jnp.bfloat16)
        copy = pltpu.make_async_copy(
            results.at[:, cols], out_ref.at[:, cols], results_out.at[number]
        )
        copy.start()
        leaving.append(copy)
    for copy in leaving:
        copy.wait()


def combine_kernel(value_ref, rows_ref, matrix_ref, out_ref):
    tokens = out_ref.shape[0]
    terms = dot(matrix_ref[...], rows_ref[...])
    mixture = terms[:tokens] + terms[tokens:]
    out_ref[...] = (value_ref[...].astype(jnp.float32) + mixture).astype(jnp.bfloat16)


def last_kernel(
    flag_ref, value_ref, rows_ref, matrix_ref, instead_ref, own_ref, back_ref, out_ref
):
    combine_kernel(value_ref, rows_ref, matrix_ref, out_ref.at[0])
    out_ref[1] = sum_of(own_ref, back_ref)

    @pl.when(flag_ref[0] != 0)
    def _():
        out_ref[0] = instead_ref[...]


def pair_combine_kernel(value_ref, rows_ref, matrix_ref, after_ref, own_ref, other_ref):
    tokens = own_ref.shape[0]
    terms = dot(matrix_ref[...], rows_ref[...])
    own = value_ref[...].astype(jnp.float32) + terms[:tokens] + terms[tokens : 2 * tokens]
    own_ref[...] = own.astype(own_ref.dtype)
    other = terms[2 * tokens : 3 * tokens] + terms[3 * tokens :]
    other_ref[...] = other.astype(jnp.bfloat16)


def other_kernel(rows_ref, matrix_ref, after_ref, out_ref):
    tokens = out_ref.shape[0]
    terms = dot(matrix_ref[...], rows_ref[...])
    out_ref[...] = (terms[:tokens] + terms[tokens:]).astype(jnp.bfloat16)


def own_kernel(value_ref, rows_ref, matrix_ref, after_ref, out_ref):
    tokens = out_ref.shape[0]
    terms = dot(matrix_ref[...], rows_ref[...])
    total = value_ref[...].astype(jnp.float32) + terms[:tokens] + terms[tokens:]
    out_ref[...] = total.astype(out_ref.dtype)


def halves_kernel(rows_ref, early_ref, late_ref):
    middle = early_ref.shape[0]
    early_ref[...] = rows_ref[:middle]
    late_ref[...] = rows_ref[middle:]


def add_kernel(own_ref, early_ref, late_ref, after_ref, out_ref):
    for number, back_ref in enumerate((early_ref, late_ref)):

        @pl.when(pl.program_id(0) == number)
        def _():
            out_ref[...] = sum_of(own_ref, back_ref)


def block_of(value, width):
    whole, index = value
    rows = whole.shape[-2]
    lead = len(index)
    return pl.BlockSpec((None,) * lead + (rows, width), lambda step: index + (0, step))


def all_of(value):
    whole, index = value
    lead = len(index)
    return pl.BlockSpec((None,) * lead + whole.shape[-2:], lambda step: index + (0, 0))


def plan(capacity, ids, weights, other_ids, other_weights, after):
    tokens = ids.shape[-1]
    lean, wide = EXPERTS * capacity, EXPERTS * 2 * capacity
    shapes = (
        (4 * tokens, wide),
        (2 * tokens, lean),
        (lean, tokens),
        (wide, 2 * tokens),
        (4 * tokens, wide),
        (2 * tokens, lean),
    )
    return pl.pallas_call(
        functools.partial(plan_kernel, capacity),
        grid=(1,),
        out_shape=[array(*shape) for shape in shapes],
        in_specs=[VMEM] * 4 + [ANY],
        out_specs=[pl.BlockSpec(shape, lambda step: (0, 0)) for shape in shapes],
        compiler_params=params(),
    )(ids, weights, other_ids, other_weights, after)


def pack(kernel, values, room, gain, others, scratch=(), flag=None, summed=False, work=0, parts=2):
    rows, width = values[0][0].shape[-2:]
    block = split(width, parts)
    packed = pl.BlockSpec((room, block), lambda step: (0, step))
    whole = pl.BlockSpec((rows, width), lambda step: (0, 0))
    picks = flag is not None
    return pl.pallas_call(
        kernel,
        grid=(width // block,),
        out_shape=(array(rows, width), array(room, width)) if summed else array(room, width),
        in_specs=[SMEM] * picks
        + [all_of(value) for value in values]
        + [all_of(gain)]
        + [spec for _, spec in others],
        out_specs=(whole, packed) if summed else packed,
        scratch_shapes=scratch,
        compiler_params=params(),
        cost_estimate=pl.CostEstimate(flops=work, bytes_accessed=0, transcendentals=0)
        if work
        else None,
    )(*[flag] * picks, *[value[0] for value in values], gain[0], *[other for other, _ in others])


def combine(value, rows, matrix):
    width = rows.shape[1]
    tokens = matrix.shape[0] // 2
    block = split(width, 2)
    return pl.pallas_call(
        combine_kernel,
        grid=(width // block,),
        out_shape=array(tokens, width),
        in_specs=[block_of(value, block), block_of((rows, ()), block), VMEM],
        out_specs=pl.BlockSpec((tokens, block), lambda step: (0, step)),
        compiler_params=params(),
    )(value[0], rows, matrix)


def last(flag, value, rows, matrix, instead, own, back):
    width = rows.shape[1]
    tokens = matrix.shape[0] // 2
    block = split(width, 2)
    part = pl.BlockSpec((tokens, block), lambda step: (0, step))
    return pl.pallas_call(
        last_kernel,
        grid=(width // block,),
        out_shape=array(2, 1, tokens, width),
        in_specs=[SMEM, part, block_of((rows, ()), block), VMEM, part, part, part],
        out_specs=pl.BlockSpec((2, None, tokens, block), lambda step: (0, 0, 0, step)),
        compiler_params=params(),
    )(flag, value, rows, matrix, instead, own, back)


def pair_combine(value, rows, matrix, after, kind):
    width = rows.shape[1]
    tokens = matrix.shape[0] // 4
    block = split(width, 2)
    part = pl.BlockSpec((tokens, block), lambda step: (0, step))
    return pl.pallas_call(
        pair_combine_kernel,
        grid=(width // block,),
        out_shape=(array(tokens, width, dtype=kind), array(tokens, width)),
        in_specs=[block_of(value, block), block_of((rows, ()), block), VMEM, ANY],
        out_specs=(part, part),
        compiler_params=params(),
    )(value[0], rows, matrix, after)


def other_then_own(value, rows, matrix, after, kind):
    room, width = rows.shape
    tokens = matrix.shape[0] // 4
    block = split(width, 2)
    part = pl.BlockSpec((tokens, block), lambda step: (0, step))

    def weights_at(number):
        return pl.BlockSpec((2 * tokens, room), lambda step: (number, 0))

    other = pl.pallas_call(
        other_kernel,
        grid=(width // block,),
        out_shape=array(tokens, width),
        in_specs=[block_of((rows, ()), block), weights_at(1), ANY],
        out_specs=part,
        compiler_params=params(),
    )(rows, matrix, after)
    own = pl.pallas_call(
        own_kernel,
        grid=(width // block,),
        out_shape=array(tokens, width, dtype=kind),
        in_specs=[block_of(value, block), block_of((rows, ()), block), weights_at(0), ANY],
        out_specs=part,
        compiler_params=params(),
    )(value[0], rows, matrix, other)
    return own, other


def halves(rows):
    count, width = rows.shape
    block = split(width, 2)
    half = pl.BlockSpec((count // 2, block), lambda step: (0, step))
    return pl.pallas_call(
        halves_kernel,
        grid=(width // block,),
        out_shape=(array(count // 2, width),) * 2,
        in_specs=[pl.BlockSpec((count, block), lambda step: (0, step))],
        out_specs=(half, half),
        compiler_params=params(),
    )(rows)


def add(own, early, late, after):
    rows, width = early.shape
    half = pl.BlockSpec((rows, width), lambda step: (step, 0))
    whole = pl.BlockSpec((rows, width), lambda step: (0, 0))
    return pl.pallas_call(
        add_kernel,
        grid=(2,),
        out_shape=array(*own.shape),
        in_specs=[half, whole, whole, ANY],
        out_specs=half,
        compiler_params=params(),
    )(own, early, late, after)


def pieces(width, sizes):
    unit = width // 7
    if width % 7 or unit % 128:
        return [slice(0, width)]
    sizes = [size * unit for size in sizes]
    starts = [sum(sizes[:number]) for number in range(len(sizes))]
    return [slice(start, start + size) for start, size in zip(starts, sizes)]


def expert_pass(rows, leg, gate_cols, up_cols, down_rows, after, work):
    count, width = rows.shape
    hidden = gate_cols.shape[-1]
    deep = pieces(width, (1, 2, 2, 2) if count > 512 else (1,) * 7)
    wide = pieces(width, (2, 2, 2, 1))
    arrivals = pltpu.SemaphoreType.DMA((len(deep),))
    return pl.pallas_call(
        functools.partial(expert_kernel, leg, deep, wide),
        out_shape=array(count, width),
        in_specs=[ANY] * 5,
        out_specs=ANY,
        scratch_shapes=(
            pltpu.VMEM((count, width), jnp.bfloat16),
            pltpu.VMEM((width, hidden), jnp.bfloat16),
            pltpu.VMEM((width, hidden), jnp.bfloat16),
            pltpu.VMEM((hidden, width), jnp.bfloat16),
            pltpu.VMEM((count, width), jnp.bfloat16),
            pltpu.VMEM((count, hidden), jnp.float32),
            pltpu.VMEM((count, hidden), jnp.float32),
            pltpu.VMEM((count, hidden), jnp.bfloat16),
            arrivals,
            arrivals,
            arrivals,
            arrivals,
            arrivals,
        ),
        compiler_params=params(),
        cost_estimate=pl.CostEstimate(flops=work, bytes_accessed=0, transcendentals=0),
    )(rows, gate_cols, up_cols, down_rows, after)


def on_device(in_flight, routes, gate_weights, norm_gain, w_gate, w_up, w_down):
    section_count = lax.axis_size("pp")
    section_pos = lax.axis_index("pp")
    tokens, top_count = routes.shape[-2:]
    width = in_flight.shape[-1]
    capacity = tokens * top_count * 5 // (4 * EXPERTS)
    down = (in_flight, (0, 0))
    up = (in_flight, (1, 0))
    down_other = other_half(in_flight[0, 0])
    ids = jnp.swapaxes(routes[:, :, 0], -1, -2)
    weights = jnp.swapaxes(gate_weights[:, :, 0], -1, -2)
    other_ids = other_half(ids)
    other_weights = other_half(weights)
    gains = norm_gain[:, :, None]

    def experts(rows, leg, after, work):
        return expert_pass(rows, leg, w_gate, w_up, w_down, after, work)

    def worked(wide, wide_packed, lean, lean_own):
        wide_rows = within_column(wide_packed)
        early, late = halves(lean_own)
        early, late = other_half(early), other_half(late)
        part_own = experts(lean_own, lean, ids, 1)
        part_early = experts(early, lean, part_own, 1)
        wide_out = experts(wide_rows, wide, part_early, 1)
        part_late = experts(late, lean, wide_out, WORK)
        return within_column(wide_out), part_own, other_half(part_early), other_half(part_late)

    lean_rows, wide_rows = EXPERTS * capacity, EXPERTS * 2 * capacity
    packed = pack(
        functools.partial(lean_pack_kernel, (0, 1), capacity),
        [up],
        lean_rows,
        (gains, (1, 0)),
        [(ids, VMEM)],
        (pltpu.VMEM((tokens, width), jnp.bfloat16), pltpu.VMEM((lean_rows, tokens), jnp.bfloat16)),
    )
    lean_own = within_column(packed)
    packed = pack(
        functools.partial(wide_pack_kernel, (0, 0), capacity),
        [down, (down_other, ())],
        wide_rows,
        (gains, (0, 0)),
        [(ids, VMEM), (other_ids, VMEM), (other_weights, ANY)],
        (
            pltpu.VMEM((2 * tokens, width), jnp.bfloat16),
            pltpu.VMEM((wide_rows, 2 * tokens), jnp.bfloat16),
        ),
    )
    wide_back, part_own, early, late = worked(0, packed, 1, lean_own)
    plans = plan(capacity, ids, weights, other_ids, other_weights, part_own)
    wide_first, lean_first, lean_matrix, wide_matrix_next, wide_second, lean_second = plans
    lean_out = add(part_own, early, late, wide_first)
    lean_back = within_column(lean_out)
    own, other = pair_combine(down, wide_back, wide_first, lean_out, jnp.bfloat16)
    own_down, other_down = moved(own, 1, 0), moved(other, 1, 1)
    own_turned, other_turned = moved(own, 0, 1), moved(other, 0, 1)
    first_up = combine(up, lean_back, lean_first)
    descending, packed = pack(
        sum_pack_kernel,
        [(own_down, ()), (other_down, ())],
        lean_rows,
        (gains, (0, 0)),
        [(lean_matrix, VMEM), (first_up, ANY), (own_turned, ANY), (other_turned, ANY)],
        (pltpu.VMEM((tokens, width), jnp.bfloat16),),
        summed=True,
        parts=1,
    )
    lean_own = within_column(packed)
    folds = (section_pos == section_count - 1).astype(jnp.int32).reshape(1)
    turned, packed = pack(
        either_pack_kernel,
        [
            (value, ())
            for value in (
                moved(first_up, -1, 0),
                moved(first_up, -1, 1),
                own,
                other_turned,
                own_turned,
                other,
            )
        ],
        wide_rows,
        (gains, (1, 0)),
        [(wide_matrix_next, VMEM)],
        (pltpu.VMEM((2 * tokens, width), jnp.bfloat16),),
        flag=folds,
        summed=True,
        work=WORK,
    )
    wide_back, part_own, early, late = worked(1, packed, 0, lean_own)
    lean_out = add(part_own, early, late, wide_second)
    lean_back = within_column(lean_out)
    own, other = other_then_own((turned, ()), wide_back, wide_second, lean_out, jnp.float32)
    starts = (section_pos == 0).astype(jnp.int32).reshape(1)
    return last(starts, descending, lean_back, lean_second, first_up, own, other_half(other))


def solution(mesh):
    placed = (
        P(None, "pp", "ep", None),
        P(None, None, "pp", "ep", None),
        P(None, None, "pp", "ep", None),
        P(None, "pp", None),
        P(None, "pp", None, "ep"),
        P(None, "pp", None, "ep"),
        P(None, "pp", "ep", None),
    )
    return jax.shard_map(
        on_device, mesh=mesh, in_specs=placed, out_specs=P(None, "pp", "ep", None), check_vma=False
    )
```

```python
import functools

import jax
import jax.numpy as jnp
from jax import lax
from jax.experimental import pallas as pl
from jax.experimental.pallas import tpu as pltpu
from jax.sharding import PartitionSpec as P

SIDE = 4
COLUMNS = (
    [SIDE * z + x for z in range(SIDE) for x in (0, 3)],
    [SIDE * z + x for z in range(SIDE) for x in (1, 2)],
)
EXPERTS = 2 * SIDE
ROOM = 127 * 2**19
WORK = 5 * 10**10
VMEM = pl.BlockSpec(memory_space=pltpu.VMEM)
SMEM = pl.BlockSpec(memory_space=pltpu.SMEM)
ANY = pl.BlockSpec(memory_space=pl.ANY)


def moved(value, steps, crossed):
    sections, places = lax.axis_size("pp"), lax.axis_size("ep")
    if steps == 0:
        sources = [sections - 1]
    else:
        sources = [section for section in range(sections) if 0 <= section + steps < sections]
    pairs = [
        (section * places + place, (section + steps) * places + (place ^ crossed))
        for section in sources
        for place in range(places)
    ]
    return lax.ppermute(value, ("pp", "ep"), pairs)


def other_half(value):
    return lax.ppermute(value, "ep", [(place, place ^ 1) for place in range(lax.axis_size("ep"))])


def within_column(rows):
    shape = rows.shape
    received = lax.all_to_all(
        rows.reshape(EXPERTS, shape[0] // EXPERTS, shape[1]),
        "ep",
        split_axis=0,
        concat_axis=0,
        tiled=True,
        axis_index_groups=COLUMNS,
    )
    return received.reshape(shape)


def iota(shape, dim):
    return lax.broadcasted_iota(jnp.int32, shape, dim)


def dot(left, right):
    return jnp.dot(left, right, preferred_element_type=jnp.float32)


def array(*shape, dtype=jnp.bfloat16):
    return jax.ShapeDtypeStruct(shape, dtype)


def split(width, parts):
    return width // parts if width % (128 * parts) == 0 else width


def params():
    return pltpu.CompilerParams(vmem_limit_bytes=ROOM)


def normalise(value, gain):
    widened = value.astype(jnp.float32)
    scale = lax.rsqrt(jnp.mean(widened * widened, axis=-1, keepdims=True) + 1e-06)
    return (widened * scale * gain).astype(jnp.bfloat16)


def slots(ids):
    tokens = ids.shape[1]
    expert = iota((EXPERTS, tokens), 0)
    named = (ids[0:1] == expert) | (ids[1:2] == expert)
    before = (iota((tokens, tokens), 0) < iota((tokens, tokens), 1)).astype(jnp.bfloat16)
    earlier = dot(jnp.where(named, 1.0, 0.0).astype(jnp.bfloat16), before)
    return jnp.where(named, earlier, -1.0)


def slot_matrix(ids, capacity, first, room, weights=None):
    tokens = ids.shape[1]
    slot = slots(ids)
    place = iota((EXPERTS, room, tokens), 1).astype(jnp.float32) - float(first)
    if weights is None:
        value = 1.0
    else:
        expert = iota((EXPERTS, tokens), 0)
        value = jnp.where(ids[0:1] == expert, weights[0:1], 0.0) + jnp.where(
            ids[1:2] == expert, weights[1:2], 0.0
        )
        value = value[:, None, :]
    chosen = (slot[:, None, :] == place) & (place >= 0.0)
    return jnp.where(chosen, value, 0.0).reshape(EXPERTS * room, tokens)


def two_terms(matrix):
    high = matrix.astype(jnp.bfloat16)
    return high, (matrix - high.astype(jnp.float32)).astype(jnp.bfloat16)


def across(matrix):
    rows, tokens = matrix.shape
    extra = -rows % 128
    if extra:
        matrix = jnp.concatenate([matrix, jnp.zeros((extra, tokens), matrix.dtype)], axis=0)
    return matrix.T[:, :rows]


def wide_matrix(ids, other_ids, capacity):
    room = 2 * capacity
    own = slot_matrix(ids, capacity, 0, room)
    other = slot_matrix(other_ids, capacity, capacity, room)
    return jnp.concatenate([own, other], axis=1).astype(jnp.bfloat16)


def lean_weight_matrix(ids, weights, capacity):
    return jnp.concatenate(
        two_terms(across(slot_matrix(ids, capacity, 0, capacity, weights))), axis=0
    )


def wide_weight_matrix(ids, weights, other_ids, other_weights, capacity):
    room = 2 * capacity
    own = two_terms(across(slot_matrix(ids, capacity, 0, room, weights)))
    other = two_terms(across(slot_matrix(other_ids, capacity, capacity, room, other_weights)))
    return jnp.concatenate(own + other, axis=0)


def plan_kernel(
    capacity,
    ids_ref,
    weights_ref,
    other_ids_ref,
    other_weights_ref,
    after_ref,
    wide_first,
    lean_first,
    lean_rows,
    wide_rows,
    wide_second,
    lean_second,
):
    def wide(tick):
        place = (tick, tick)
        return wide_weight_matrix(
            ids_ref[place],
            weights_ref[place],
            other_ids_ref[place],
            other_weights_ref[place],
            capacity,
        )

    def lean(tick):
        place = (tick, 1 - tick)
        return lean_weight_matrix(ids_ref[place], weights_ref[place], capacity)

    wide_first[...], lean_first[...] = wide(0), lean(0)
    wide_second[...], lean_second[...] = wide(1), lean(1)
    lean_rows[...] = slot_matrix(ids_ref[1, 0], capacity, 0, capacity).astype(jnp.bfloat16)
    wide_rows[...] = wide_matrix(ids_ref[1, 1], other_ids_ref[1, 1], capacity)


def spread(matrix_ref, normed_ref, out_ref):
    width = out_ref.shape[1]
    cols = pl.ds(pl.multiple_of(pl.program_id(0) * width, 128), width)
    out_ref[...] = dot(matrix_ref[...], normed_ref[:, cols]).astype(jnp.bfloat16)


def sum_of(first_ref, second_ref):
    total = first_ref[...].astype(jnp.float32) + second_ref[...].astype(jnp.float32)
    return total.astype(jnp.bfloat16)


def lean_pack_kernel(where, capacity, value_ref, gain_ref, ids_ref, out_ref, normed_ref, matrix_ref):
    @pl.when(pl.program_id(0) == 0)
    def _():
        normed_ref[...] = normalise(value_ref[...], gain_ref[...])
        matrix_ref[...] = slot_matrix(ids_ref[where], capacity, 0, capacity).astype(jnp.bfloat16)

    spread(matrix_ref, normed_ref, out_ref)


def sum_pack_kernel(
    first_ref,
    second_ref,
    gain_ref,
    matrix_ref,
    after_ref,
    own_turned_ref,
    other_turned_ref,
    value_ref,
    out_ref,
    normed_ref,
):
    @pl.when(pl.program_id(0) == 0)
    def _():
        value_ref[...] = sum_of(first_ref, second_ref)
        normed_ref[...] = normalise(value_ref[...], gain_ref[...])

    spread(matrix_ref, normed_ref, out_ref)


def wide_pack_kernel(
    where,
    capacity,
    own_ref,
    other_ref,
    gain_ref,
    ids_ref,
    other_ids_ref,
    after_ref,
    out_ref,
    normed_ref,
    matrix_ref,
):
    @pl.when(pl.program_id(0) == 0)
    def _():
        tokens = own_ref.shape[0]
        normed_ref[:tokens] = normalise(own_ref[...], gain_ref[...])
        normed_ref[tokens:] = normalise(other_ref[...], gain_ref[...])
        matrix_ref[...] = wide_matrix(ids_ref[where], other_ids_ref[where], capacity)

    spread(matrix_ref, normed_ref, out_ref)


def either_pack_kernel(
    flag_ref,
    own_ref,
    other_ref,
    own_first_ref,
    own_second_ref,
    other_first_ref,
    other_second_ref,
    gain_ref,
    matrix_ref,
    value_ref,
    out_ref,
    normed_ref,
):
    first = pl.program_id(0) == 0
    tokens = own_ref.shape[0]

    @pl.when(first & (flag_ref[0] == 0))
    def _():
        value_ref[...] = own_ref[...]
        normed_ref[:tokens] = normalise(own_ref[...], gain_ref[...])
        normed_ref[tokens:] = normalise(other_ref[...], gain_ref[...])

    @pl.when(first & (flag_ref[0] != 0))
    def _():
        value_ref[...] = sum_of(own_first_ref, own_second_ref)
        normed_ref[:tokens] = normalise(value_ref[...], gain_ref[...])
        normed_ref[tokens:] = normalise(sum_of(other_first_ref, other_second_ref), gain_ref[...])

    spread(matrix_ref, normed_ref, out_ref)


def expert_kernel(
    leg,
    deep,
    wide,
    rows_ref,
    gate_ref,
    up_ref,
    down_ref,
    after_ref,
    out_ref,
    rows,
    gate_cols,
    up_cols,
    down_rows,
    results,
    gate_sum,
    up_sum,
    active,
    rows_in,
    gate_in,
    up_in,
    down_in,
    results_out,
):
    arriving = []
    for number, cols in enumerate(deep):
        arriving.append(
            (
                pltpu.make_async_copy(rows_ref.at[:, cols], rows.at[:, cols], rows_in.at[number]),
                pltpu.make_async_copy(
                    gate_ref.at[leg, 0, cols], gate_cols.at[cols], gate_in.at[number]
                ),
                pltpu.make_async_copy(up_ref.at[leg, 0, cols], up_cols.at[cols], up_in.at[number]),
            )
        )
    for number, cols in enumerate(wide):
        arriving.append(
            (
                pltpu.make_async_copy(
                    down_ref.at[leg, 0, :, cols], down_rows.at[:, cols], down_in.at[number]
                ),
            )
        )
    for copies in arriving:
        for copy in copies:
            copy.start()
    for number, cols in enumerate(deep):
        for copy in arriving[number]:
            copy.wait()
        gate = dot(rows[:, cols], gate_cols[cols])
        up = dot(rows[:, cols], up_cols[cols])
        if number > 0:
            gate = gate + gate_sum[...]
            up = up + up_sum[...]
        if number < len(deep) - 1:
            gate_sum[...] = gate
            up_sum[...] = up
        else:
            active[...] = (jax.nn.silu(gate) * up).astype(jnp.bfloat16)
    leaving = []
    for number, cols in enumerate(wide):
        for copy in arriving[len(deep) + number]:
            copy.wait()
        results[:, cols] = dot(active[...], down_rows[:, cols]).astype(jnp.bfloat16)
        copy = pltpu.make_async_copy(
            results.at[:, cols], out_ref.at[:, cols], results_out.at[number]
        )
        copy.start()
        leaving.append(copy)
    for copy in leaving:
        copy.wait()


def combine_kernel(value_ref, rows_ref, matrix_ref, out_ref):
    tokens = out_ref.shape[0]
    terms = dot(matrix_ref[...], rows_ref[...])
    mixture = terms[:tokens] + terms[tokens:]
    out_ref[...] = (value_ref[...].astype(jnp.float32) + mixture).astype(jnp.bfloat16)


def last_kernel(
    flag_ref, value_ref, rows_ref, matrix_ref, instead_ref, own_ref, back_ref, out_ref
):
    combine_kernel(value_ref, rows_ref, matrix_ref, out_ref.at[0])
    out_ref[1] = sum_of(own_ref, back_ref)

    @pl.when(flag_ref[0] != 0)
    def _():
        out_ref[0] = instead_ref[...]


def pair_combine_kernel(value_ref, rows_ref, matrix_ref, after_ref, own_ref, other_ref):
    tokens = own_ref.shape[0]
    terms = dot(matrix_ref[...], rows_ref[...])
    own = value_ref[...].astype(jnp.float32) + terms[:tokens] + terms[tokens : 2 * tokens]
    own_ref[...] = own.astype(own_ref.dtype)
    other = terms[2 * tokens : 3 * tokens] + terms[3 * tokens :]
    other_ref[...] = other.astype(jnp.bfloat16)


def other_kernel(rows_ref, matrix_ref, after_ref, out_ref):
    tokens = out_ref.shape[0]
    terms = dot(matrix_ref[...], rows_ref[...])
    out_ref[...] = (terms[:tokens] + terms[tokens:]).astype(jnp.bfloat16)


def own_kernel(value_ref, rows_ref, matrix_ref, after_ref, out_ref):
    tokens = out_ref.shape[0]
    terms = dot(matrix_ref[...], rows_ref[...])
    total = value_ref[...].astype(jnp.float32) + terms[:tokens] + terms[tokens:]
    out_ref[...] = total.astype(out_ref.dtype)


def halves_kernel(rows_ref, early_ref, late_ref):
    middle = early_ref.shape[0]
    early_ref[...] = rows_ref[:middle]
    late_ref[...] = rows_ref[middle:]


def add_kernel(own_ref, early_ref, late_ref, after_ref, out_ref):
    for number, back_ref in enumerate((early_ref, late_ref)):

        @pl.when(pl.program_id(0) == number)
        def _():
            out_ref[...] = sum_of(own_ref, back_ref)


def block_of(value, width):
    whole, index = value
    rows = whole.shape[-2]
    lead = len(index)
    return pl.BlockSpec((None,) * lead + (rows, width), lambda step: index + (0, step))


def all_of(value):
    whole, index = value
    lead = len(index)
    return pl.BlockSpec((None,) * lead + whole.shape[-2:], lambda step: index + (0, 0))


def plan(capacity, ids, weights, other_ids, other_weights, after):
    tokens = ids.shape[-1]
    lean, wide = EXPERTS * capacity, EXPERTS * 2 * capacity
    shapes = (
        (4 * tokens, wide),
        (2 * tokens, lean),
        (lean, tokens),
        (wide, 2 * tokens),
        (4 * tokens, wide),
        (2 * tokens, lean),
    )
    return pl.pallas_call(
        functools.partial(plan_kernel, capacity),
        grid=(1,),
        out_shape=[array(*shape) for shape in shapes],
        in_specs=[VMEM] * 4 + [ANY],
        out_specs=[pl.BlockSpec(shape, lambda step: (0, 0)) for shape in shapes],
        compiler_params=params(),
    )(ids, weights, other_ids, other_weights, after)


def pack(kernel, values, room, gain, others, scratch=(), flag=None, summed=False, work=0):
    rows, width = values[0][0].shape[-2:]
    block = split(width, 2)
    packed = pl.BlockSpec((room, block), lambda step: (0, step))
    whole = pl.BlockSpec((rows, width), lambda step: (0, 0))
    picks = flag is not None
    return pl.pallas_call(
        kernel,
        grid=(width // block,),
        out_shape=(array(rows, width), array(room, width)) if summed else array(room, width),
        in_specs=[SMEM] * picks
        + [all_of(value) for value in values]
        + [all_of(gain)]
        + [spec for _, spec in others],
        out_specs=(whole, packed) if summed else packed,
        scratch_shapes=scratch,
        compiler_params=params(),
        cost_estimate=pl.CostEstimate(flops=work, bytes_accessed=0, transcendentals=0)
        if work
        else None,
    )(*[flag] * picks, *[value[0] for value in values], gain[0], *[other for other, _ in others])


def combine(value, rows, matrix):
    width = rows.shape[1]
    tokens = matrix.shape[0] // 2
    block = split(width, 2)
    return pl.pallas_call(
        combine_kernel,
        grid=(width // block,),
        out_shape=array(tokens, width),
        in_specs=[block_of(value, block), block_of((rows, ()), block), VMEM],
        out_specs=pl.BlockSpec((tokens, block), lambda step: (0, step)),
        compiler_params=params(),
    )(value[0], rows, matrix)


def last(flag, value, rows, matrix, instead, own, back):
    width = rows.shape[1]
    tokens = matrix.shape[0] // 2
    block = split(width, 2)
    part = pl.BlockSpec((tokens, block), lambda step: (0, step))
    return pl.pallas_call(
        last_kernel,
        grid=(width // block,),
        out_shape=array(2, 1, tokens, width),
        in_specs=[SMEM, part, block_of((rows, ()), block), VMEM, part, part, part],
        out_specs=pl.BlockSpec((2, None, tokens, block), lambda step: (0, 0, 0, step)),
        compiler_params=params(),
    )(flag, value, rows, matrix, instead, own, back)


def pair_combine(value, rows, matrix, after, kind):
    width = rows.shape[1]
    tokens = matrix.shape[0] // 4
    block = split(width, 2)
    part = pl.BlockSpec((tokens, block), lambda step: (0, step))
    return pl.pallas_call(
        pair_combine_kernel,
        grid=(width // block,),
        out_shape=(array(tokens, width, dtype=kind), array(tokens, width)),
        in_specs=[block_of(value, block), block_of((rows, ()), block), VMEM, ANY],
        out_specs=(part, part),
        compiler_params=params(),
    )(value[0], rows, matrix, after)


def other_then_own(value, rows, matrix, after, kind):
    room, width = rows.shape
    tokens = matrix.shape[0] // 4
    block = split(width, 2)
    part = pl.BlockSpec((tokens, block), lambda step: (0, step))

    def weights_at(number):
        return pl.BlockSpec((2 * tokens, room), lambda step: (number, 0))

    other = pl.pallas_call(
        other_kernel,
        grid=(width // block,),
        out_shape=array(tokens, width),
        in_specs=[block_of((rows, ()), block), weights_at(1), ANY],
        out_specs=part,
        compiler_params=params(),
    )(rows, matrix, after)
    own = pl.pallas_call(
        own_kernel,
        grid=(width // block,),
        out_shape=array(tokens, width, dtype=kind),
        in_specs=[block_of(value, block), block_of((rows, ()), block), weights_at(0), ANY],
        out_specs=part,
        compiler_params=params(),
    )(value[0], rows, matrix, other)
    return own, other


def halves(rows):
    count, width = rows.shape
    block = split(width, 2)
    half = pl.BlockSpec((count // 2, block), lambda step: (0, step))
    return pl.pallas_call(
        halves_kernel,
        grid=(width // block,),
        out_shape=(array(count // 2, width),) * 2,
        in_specs=[pl.BlockSpec((count, block), lambda step: (0, step))],
        out_specs=(half, half),
        compiler_params=params(),
    )(rows)


def add(own, early, late, after):
    rows, width = early.shape
    half = pl.BlockSpec((rows, width), lambda step: (step, 0))
    whole = pl.BlockSpec((rows, width), lambda step: (0, 0))
    return pl.pallas_call(
        add_kernel,
        grid=(2,),
        out_shape=array(*own.shape),
        in_specs=[half, whole, whole, ANY],
        out_specs=half,
        compiler_params=params(),
    )(own, early, late, after)


def pieces(width, sizes):
    unit = width // 7
    if width % 7 or unit % 128:
        return [slice(0, width)]
    sizes = [size * unit for size in sizes]
    starts = [sum(sizes[:number]) for number in range(len(sizes))]
    return [slice(start, start + size) for start, size in zip(starts, sizes)]


def expert_pass(rows, leg, gate_cols, up_cols, down_rows, after, work):
    count, width = rows.shape
    hidden = gate_cols.shape[-1]
    deep = pieces(width, (1, 2, 2, 2) if count > 512 else (1,) * 7)
    wide = pieces(width, (2, 2, 2, 1))
    arrivals = pltpu.SemaphoreType.DMA((len(deep),))
    return pl.pallas_call(
        functools.partial(expert_kernel, leg, deep, wide),
        out_shape=array(count, width),
        in_specs=[ANY] * 5,
        out_specs=ANY,
        scratch_shapes=(
            pltpu.VMEM((count, width), jnp.bfloat16),
            pltpu.VMEM((width, hidden), jnp.bfloat16),
            pltpu.VMEM((width, hidden), jnp.bfloat16),
            pltpu.VMEM((hidden, width), jnp.bfloat16),
            pltpu.VMEM((count, width), jnp.bfloat16),
            pltpu.VMEM((count, hidden), jnp.float32),
            pltpu.VMEM((count, hidden), jnp.float32),
            pltpu.VMEM((count, hidden), jnp.bfloat16),
            arrivals,
            arrivals,
            arrivals,
            arrivals,
            arrivals,
        ),
        compiler_params=params(),
        cost_estimate=pl.CostEstimate(flops=work, bytes_accessed=0, transcendentals=0),
    )(rows, gate_cols, up_cols, down_rows, after)


def on_device(in_flight, routes, gate_weights, norm_gain, w_gate, w_up, w_down):
    section_count = lax.axis_size("pp")
    section_pos = lax.axis_index("pp")
    tokens, top_count = routes.shape[-2:]
    width = in_flight.shape[-1]
    capacity = tokens * top_count * 5 // (4 * EXPERTS)
    down = (in_flight, (0, 0))
    up = (in_flight, (1, 0))
    down_other = other_half(in_flight[0, 0])
    ids = jnp.swapaxes(routes[:, :, 0], -1, -2)
    weights = jnp.swapaxes(gate_weights[:, :, 0], -1, -2)
    other_ids = other_half(ids)
    other_weights = other_half(weights)
    gains = norm_gain[:, :, None]

    def experts(rows, leg, after, work):
        return expert_pass(rows, leg, w_gate, w_up, w_down, after, work)

    def worked(wide, wide_packed, lean, lean_own):
        wide_rows = within_column(wide_packed)
        early, late = halves(lean_own)
        early, late = other_half(early), other_half(late)
        part_own = experts(lean_own, lean, ids, 1)
        part_early = experts(early, lean, part_own, 1)
        wide_out = experts(wide_rows, wide, part_early, 1)
        part_late = experts(late, lean, wide_out, WORK)
        return within_column(wide_out), part_own, other_half(part_early), other_half(part_late)

    lean_rows, wide_rows = EXPERTS * capacity, EXPERTS * 2 * capacity
    packed = pack(
        functools.partial(lean_pack_kernel, (0, 1), capacity),
        [up],
        lean_rows,
        (gains, (1, 0)),
        [(ids, VMEM)],
        (pltpu.VMEM((tokens, width), jnp.bfloat16), pltpu.VMEM((lean_rows, tokens), jnp.bfloat16)),
    )
    lean_own = within_column(packed)
    packed = pack(
        functools.partial(wide_pack_kernel, (0, 0), capacity),
        [down, (down_other, ())],
        wide_rows,
        (gains, (0, 0)),
        [(ids, VMEM), (other_ids, VMEM), (other_weights, ANY)],
        (
            pltpu.VMEM((2 * tokens, width), jnp.bfloat16),
            pltpu.VMEM((wide_rows, 2 * tokens), jnp.bfloat16),
        ),
    )
    wide_back, part_own, early, late = worked(0, packed, 1, lean_own)
    plans = plan(capacity, ids, weights, other_ids, other_weights, part_own)
    wide_first, lean_first, lean_matrix, wide_matrix_next, wide_second, lean_second = plans
    lean_out = add(part_own, early, late, wide_first)
    lean_back = within_column(lean_out)
    own, other = pair_combine(down, wide_back, wide_first, lean_out, jnp.bfloat16)
    own_down, other_down = moved(own, 1, 0), moved(other, 1, 1)
    own_turned, other_turned = moved(own, 0, 1), moved(other, 0, 1)
    first_up = combine(up, lean_back, lean_first)
    descending, packed = pack(
        sum_pack_kernel,
        [(own_down, ()), (other_down, ())],
        lean_rows,
        (gains, (0, 0)),
        [(lean_matrix, VMEM), (ids, ANY), (own_turned, ANY), (other_turned, ANY)],
        (pltpu.VMEM((tokens, width), jnp.bfloat16),),
        summed=True,
    )
    lean_own = within_column(packed)
    folds = (section_pos == section_count - 1).astype(jnp.int32).reshape(1)
    turned, packed = pack(
        either_pack_kernel,
        [
            (value, ())
            for value in (
                moved(first_up, -1, 0),
                moved(first_up, -1, 1),
                own,
                other_turned,
                own_turned,
                other,
            )
        ],
        wide_rows,
        (gains, (1, 0)),
        [(wide_matrix_next, VMEM)],
        (pltpu.VMEM((2 * tokens, width), jnp.bfloat16),),
        flag=folds,
        summed=True,
        work=WORK,
    )
    wide_back, part_own, early, late = worked(1, packed, 0, lean_own)
    lean_out = add(part_own, early, late, wide_second)
    lean_back = within_column(lean_out)
    own, other = other_then_own((turned, ()), wide_back, wide_second, lean_out, jnp.float32)
    starts = (section_pos == 0).astype(jnp.int32).reshape(1)
    return last(starts, descending, lean_back, lean_second, first_up, own, other_half(other))


def solution(mesh):
    placed = (
        P(None, "pp", "ep", None),
        P(None, None, "pp", "ep", None),
        P(None, None, "pp", "ep", None),
        P(None, "pp", None),
        P(None, "pp", None, "ep"),
        P(None, "pp", None, "ep"),
        P(None, "pp", "ep", None),
    )
    return jax.shard_map(
        on_device, mesh=mesh, in_specs=placed, out_specs=P(None, "pp", "ep", None), check_vma=False
    )
```
